512 devices in a mesh: blk: 16 (over x_hi, y, core), grid: 32 (over z, x_lo).
Axes of the slice: x: 4 (x_hi: 2, x_lo: 2; x = x_hi * 2 + x_lo), y: 4, z: 16, core: 2. Of those that a mesh axis runs over, the one named last changes fastest.
Arguments:
- orbitals: float32 [32, 96, 9216], P('blk', 'grid'), may hold values from -5 to 5
Outputs:
- exchange_terms: float32 [32, 96, 9216], P('blk', 'grid')
The draws below stay inside these ranges and needn't reach their ends.
All inputs are finite; a program needn't handle non-finite values.
Results may differ from the reference program's by a relative error of at most 0.000084.
Values sent between devices are 32-bit elements; how exact they have to be, the bound alone decides.
A program may use at most 64 MiB of HBM per device.

```python
import math
import jax
import jax.numpy as jnp
from jax import lax

NG = 96
ORB = 2
ORBITALS = 32
N_BLK = 16


def draw_orbitals(key, part):
    key = jax.random.fold_in(key, 7)
    shape = (ORBITALS, NG, NG * NG)
    values = jax.random.normal(key, shape, jnp.float32)
    return jnp.clip(values, -5.0, 5.0)


def setup_inputs(seed: int = 0) -> dict:
    seeds = jax.random.split(jax.random.key(seed), 2)
    return {
        "orbitals": draw_orbitals(jax.random.fold_in(seeds[1], 71), 0),
    }


BOX_LENGTH = 37.25
OMEGA = 0.11


def screened(squared):
    safe = jnp.where(squared > 0, squared, jnp.float32(1.0))
    value = 4.0 * math.pi / safe * (1.0 - jnp.exp(-safe / (4.0 * OMEGA * OMEGA)))
    return jnp.where(squared > 0, value, jnp.float32(math.pi / (OMEGA * OMEGA)))


def wavenumbers():
    indices = jnp.arange(NG, dtype=jnp.int32)
    signed = jnp.where(indices < NG - NG // 2, indices, indices - NG)
    return signed.astype(jnp.float32) * jnp.float32(2.0 * math.pi / BOX_LENGTH)


def reference(orbitals):
    blocks = orbitals.reshape(N_BLK, ORB, NG, NG, NG)
    previous = jnp.roll(blocks, 1, axis=0)
    wave = wavenumbers()
    squared = wave[:, None, None] ** 2 + wave[None, :, None] ** 2 + wave[None, None, :] ** 2
    screen = screened(squared)

    def pair_block(operands):
        own_block, partner = operands
        density = own_block[:, None] * partner[None]
        spectrum = jnp.fft.fftn(density, axes=(2, 3, 4))
        potential = jnp.real(jnp.fft.ifftn(spectrum * screen, axes=(2, 3, 4))).astype(jnp.float32)
        to_own = -jnp.einsum("ijxyz,jxyz->ixyz", potential, partner, precision=lax.Precision.HIGHEST)
        to_partner = -jnp.einsum("ijxyz,ixyz->jxyz", potential, own_block, precision=lax.Precision.HIGHEST)
        return to_own, to_partner

    to_own, to_partner = lax.map(pair_block, (blocks, previous))
    total = to_own + jnp.roll(to_partner, -1, axis=0)
    return total.reshape(ORBITALS, NG, NG * NG)
```

```python
import functools
import math

import jax
import jax.numpy as jnp
import ml_dtypes
import numpy as np
from jax import lax
from jax.experimental import pallas as pl
from jax.experimental.pallas import tpu as pltpu
from jax.sharding import PartitionSpec as P

NG = 96
LANES = 128
BOX_LENGTH = 37.25
OMEGA = 0.11
SLABS = 32
PLANES = 3
ROWS = 14
PITCH = 16
MESH = pl.DeviceIdType.MESH


def split_table(table):
    high = table.astype(ml_dtypes.bfloat16)
    low = (table - high.astype(np.float64)).astype(ml_dtypes.bfloat16)
    return np.stack([high, low])


def tables():
    index = np.arange(NG)
    angle = 2.0 * np.pi / NG * ((index[:, None] * index[None, :]) % NG)
    hartley = np.cos(angle) + np.sin(angle)
    order = (np.arange(PLANES)[:, None] + PLANES * np.arange(SLABS)[None, :]).reshape(-1)
    dealt = hartley[order]
    packed = np.zeros((2 * NG, 2 * LANES))
    for i in range(2):
        packed[i * NG : (i + 1) * NG, i * LANES : i * LANES + NG] = hartley
    to_spectrum = np.concatenate([packed.T, packed.T[:, LANES : 2 * NG]], axis=1)
    from_spectrum = np.concatenate([packed, np.zeros((2 * LANES - 2 * NG, 2 * LANES))], axis=0)
    return tuple(split_table(t) for t in (dealt, dealt.T, to_spectrum, from_spectrum))


def halves(value):
    high = value.astype(jnp.bfloat16)
    low = (value - high.astype(jnp.float32)).astype(jnp.bfloat16)
    return high, low


def dot(a, b):
    return jnp.dot(a, b, preferred_element_type=jnp.float32)


def times_table(value, table):
    high, low = halves(value)
    return dot(high, table[0]) + (dot(low, table[0]) + dot(high, table[1]))


def table_times(table, value):
    high, low = halves(value)
    return dot(table[0], high) + (dot(table[0], low) + dot(table[1], high))


def signed(index):
    return jnp.where(index < NG - NG // 2, index, index - NG).astype(jnp.float32) * jnp.float32(
        2.0 * math.pi / BOX_LENGTH
    )


def screen_tile(kx, ky, kz):
    squared = signed(kx) ** 2 + signed(ky) ** 2 + signed(kz) ** 2
    safe = jnp.where(squared > 0, squared, jnp.float32(1.0))
    value = 4.0 * math.pi / safe * (1.0 - jnp.exp(-safe / (4.0 * OMEGA * OMEGA)))
    value = jnp.where(squared > 0, value, jnp.float32(math.pi / (OMEGA * OMEGA)))
    return value * jnp.float32(1.0 / (NG * NG * NG))


def kernel(
    own, dealt, dealt_t, to_spectrum, from_spectrum, out,
    partner, sent, arrived, screened, returned, screen, terms, terms_in,
    swap_send, swap_recv, send_sem, recv_sem, local_sem,
):
    me = lax.axis_index("grid")
    block = lax.axis_index("blk")
    blocks = lax.axis_size("blk")
    after = lax.rem(block + 1, blocks)
    before = lax.rem(block + blocks - 1, blocks)

    barrier = pltpu.get_barrier_semaphore()

    def greet(k, carry):
        peer = lax.rem(me + k, SLABS)
        pl.semaphore_signal(barrier, inc=1, device_id={"grid": peer}, device_id_type=MESH)
        return carry

    pl.semaphore_signal(barrier, inc=1, device_id={"blk": before}, device_id_type=MESH)
    pl.semaphore_signal(barrier, inc=1, device_id={"blk": after}, device_id_type=MESH)
    lax.fori_loop(1, SLABS, greet, 0)

    shape = (NG, LANES)
    kx = lax.broadcasted_iota(jnp.int32, shape, 0)
    lane = lax.broadcasted_iota(jnp.int32, shape, 1)
    low_half = lane < LANES // 2
    first = PLANES * me
    for r in range(PLANES):
        screen[:, r * LANES : (r + 1) * LANES] = screen_tile(
            kx, jnp.full(shape, first + r, jnp.int32), jnp.where(lane < NG, lane, lane - NG)
        )
    kz = jnp.where(low_half, lane, lane - LANES // 2) + (LANES - NG)
    screen[:, 3 * LANES : 4 * LANES] = screen_tile(kx, jnp.where(low_half, first, first + 1), kz)
    screen[:, 4 * LANES : 5 * LANES] = screen_tile(kx, jnp.full(shape, first + 2, jnp.int32), kz)

    pl.semaphore_wait(barrier, SLABS + 1)

    def swap(source, target, slot, whom):
        return pltpu.make_async_remote_copy(
            src_ref=source, dst_ref=target, send_sem=swap_send.at[slot], recv_sem=swap_recv.at[slot],
            device_id={"blk": whom}, device_id_type=MESH,
        )

    orbital_swaps = [swap(own.at[j], partner.at[j], j, after) for j in range(2)]
    for copy in orbital_swaps:
        copy.start()

    def message(source, target, slot, k, origin, peer):
        return pltpu.make_async_remote_copy(
            src_ref=source.at[peer, pl.ds(0, ROWS)],
            dst_ref=target.at[origin, pl.ds(0, ROWS)],
            send_sem=send_sem.at[slot, k],
            recv_sem=recv_sem.at[slot, origin],
            device_id={"grid": peer},
            device_id_type=MESH,
        )

    def stay(source, target, slot):
        return pltpu.make_async_copy(source.at[me], target.at[me], local_sem.at[slot])

    def scatter(source, target, slot):
        def one(k, carry):
            message(source, target, slot, k, me, lax.rem(me + k, SLABS)).start()
            return carry

        lax.fori_loop(1, SLABS, one, 0)
        stay(source, target, slot).start()

    def gather(source, target, slot):
        def one(k, carry):
            peer = lax.rem(me + k, SLABS)
            message(source, target, slot, k, peer, peer).wait_recv()
            return carry

        lax.fori_loop(1, SLABS, one, 0)
        stay(source, target, slot).wait()

    def drain(source, target, slot):
        def one(k, carry):
            message(source, target, slot, k, me, lax.rem(me + k, SLABS)).wait_send()
            return carry

        lax.fori_loop(1, SLABS, one, 0)

    def put(ref, row, value):
        ref.reshape(SLABS * PITCH, LANES)[pl.ds(row, SLABS, stride=PITCH), :] = value

    def get(ref, row):
        return ref.reshape(SLABS * PITCH, LANES)[pl.ds(row, SLABS, stride=PITCH), :]

    in_low = lax.broadcasted_iota(jnp.int32, (SLABS, LANES), 1) < LANES // 2

    def turned(value):
        return pltpu.roll(value, LANES // 2, 1)

    for j in range(2):
        orbital_swaps[j].wait_recv()
        other = partner[j]
        density = jnp.concatenate([own[0] * other, own[1] * other], axis=1)
        along_z = times_table(density, to_spectrum)
        third = []
        for x in range(PLANES):
            spectrum = table_times(dealt, along_z[x * NG : (x + 1) * NG])
            rest = []
            for r in range(PLANES):
                rows = spectrum[r * SLABS : (r + 1) * SLABS]
                put(sent.at[j], x * 4 + r, rows[:, :LANES])
                rest.append(rows[:, LANES:])
            put(sent.at[j], x * 4 + 3, jnp.where(in_low, rest[0], rest[1]))
            third.append(rest[2])
        put(sent.at[j], 12, jnp.where(in_low, third[0], third[1]))
        put(sent.at[j], 13, third[2])
        scatter(sent.at[j], arrived.at[j], j)

    for j in range(2):
        gather(sent.at[j], arrived.at[j], j)
        columns = []
        for r in range(4):
            columns.append(jnp.concatenate([get(arrived.at[j], x * 4 + r) for x in range(PLANES)], axis=0))
        pair = get(arrived.at[j], 12)
        columns.append(jnp.concatenate([pair, turned(pair), get(arrived.at[j], 13)], axis=0))
        spectrum = table_times(dealt_t, jnp.concatenate(columns, axis=1))
        back = table_times(dealt, spectrum * screen[...])
        for x in range(PLANES):
            rows = back[x * SLABS : (x + 1) * SLABS]
            for r in range(4):
                put(screened.at[j], x * 4 + r, rows[:, r * LANES : (r + 1) * LANES])
        last = back[:, 4 * LANES :]
        put(screened.at[j], 12, jnp.where(in_low, last[:SLABS], turned(last[SLABS : 2 * SLABS])))
        put(screened.at[j], 13, last[2 * SLABS :])
        scatter(screened.at[j], returned.at[j], 2 + j)

    term_swaps = [swap(terms.at[j], terms_in.at[j], 2 + j, before) for j in range(2)]
    for j in range(2):
        gather(screened.at[j], returned.at[j], 2 + j)
        pair = get(returned.at[j], 12)
        third = [pair, turned(pair), get(returned.at[j], 13)]
        planes = []
        for x in range(PLANES):
            main = jnp.concatenate([get(returned.at[j], x * 4 + r) for r in range(PLANES)], axis=0)
            both = get(returned.at[j], x * 4 + 3)
            rest = jnp.concatenate([both, turned(both), third[x]], axis=0)
            planes.append(table_times(dealt_t, jnp.concatenate([main, rest], axis=1)))
        potential = times_table(jnp.concatenate(planes, axis=0), from_spectrum)
        first_own, second_own = potential[:, :LANES], potential[:, LANES:]
        terms[j] = -(first_own * own[0] + second_own * own[1])
        term_swaps[j].start()
        other = partner[j]
        if j == 0:
            out[0] = -(first_own * other)
            out[1] = -(second_own * other)
        else:
            out[0] = out[0] - first_own * other
            out[1] = out[1] - second_own * other
    for j in range(2):
        term_swaps[j].wait_recv()
        out[j] = out[j] + terms_in[j]

    for copy in orbital_swaps + term_swaps:
        copy.wait_send()
    for j in range(2):
        drain(sent.at[j], arrived.at[j], j)
        drain(screened.at[j], returned.at[j], 2 + j)


def on_device(orbitals):
    count, planes, cells = orbitals.shape
    own = orbitals.reshape(count, planes * NG, NG)
    own = jnp.pad(own, ((0, 0), (0, 0), (0, LANES - NG)))
    vmem = pl.BlockSpec(memory_space=pltpu.VMEM)
    grid_rows = planes * NG
    messages = pltpu.VMEM((2, SLABS, PITCH, LANES), jnp.float32)
    pair = pltpu.VMEM((2, grid_rows, LANES), jnp.float32)
    terms = pl.pallas_call(
        kernel,
        out_shape=jax.ShapeDtypeStruct((count, grid_rows, LANES), jnp.float32),
        in_specs=[vmem] * 5,
        out_specs=vmem,
        scratch_shapes=[
            pair, messages, messages, messages, messages,
            pltpu.VMEM((NG, 5 * LANES), jnp.float32), pair, pair,
            pltpu.SemaphoreType.DMA((4,)), pltpu.SemaphoreType.DMA((4,)),
            pltpu.SemaphoreType.DMA((4, SLABS)), pltpu.SemaphoreType.DMA((4, SLABS)),
            pltpu.SemaphoreType.DMA((4,)),
        ],
        compiler_params=pltpu.CompilerParams(
            collective_id=0, has_side_effects=True, vmem_limit_bytes=48 * 1024 * 1024
        ),
    )(own, *tables())
    return terms[:, :, :NG].reshape(count, planes, cells)


def solution(mesh):
    spec = P("blk", "grid", None)
    return jax.shard_map(on_device, mesh=mesh, in_specs=(spec,), out_specs=spec, check_vma=False)
```

```python
import math

import jax
import jax.numpy as jnp
import numpy as np
from jax import lax
from jax.experimental import pallas as pl
from jax.experimental.pallas import tpu as pltpu
from jax.sharding import PartitionSpec as P

NG = 96
LANES = 128
HALF = LANES // 2
BOX_LENGTH = 37.25
OMEGA = 0.11
SLABS = 32
PLANES = 3
TILES = NG * NG // LANES
TURN = 4
TURNS = NG // TURN
MAIN = 4 * PLANES
MAIN_PITCH = 16
REST = PLANES
REST_PITCH = 8
MESH = pl.DeviceIdType.MESH
FAR_FIRST = sorted(range(1, SLABS), key=lambda k: abs(k - SLABS // 2))


def tables():
    index = np.arange(NG)
    angle = 2.0 * np.pi / NG * ((index[:, None] * index[None, :]) % NG)
    hartley = np.cos(angle) + np.sin(angle)
    by_slab = (np.arange(PLANES)[:, None] + PLANES * np.arange(SLABS)[None, :]).reshape(-1)
    by_turn = (np.arange(TURN)[:, None] + TURN * np.arange(TURNS)[None, :]).reshape(-1)
    dealt = hartley[by_slab][:, by_turn]
    packed = np.zeros((2 * NG, 2 * LANES))
    for i in range(2):
        packed[i * NG : (i + 1) * NG, i * LANES : i * LANES + NG] = hartley
    to_spectrum = np.concatenate([packed.T, packed.T[:, LANES : 2 * NG]], axis=1)
    from_spectrum = np.concatenate([packed, np.zeros((2 * LANES - 2 * NG, 2 * LANES))], axis=0)
    return tuple(t.astype(np.float32) for t in (dealt, dealt.T, to_spectrum, from_spectrum))


def halves(value):
    high = value.astype(jnp.bfloat16)
    low = (value - high.astype(jnp.float32)).astype(jnp.bfloat16)
    return high, low


def dot(a, b):
    return jnp.dot(a, b, preferred_element_type=jnp.float32)


def times_table(value, table):
    high, low = halves(value)
    return dot(high, table[0]) + (dot(low, table[0]) + dot(high, table[1]))


def table_times(table, value):
    high, low = halves(value)
    return dot(table[0], high) + (dot(table[0], low) + dot(table[1], high))


def signed(index):
    return jnp.where(index < NG - NG // 2, index, index - NG).astype(jnp.float32) * jnp.float32(
        2.0 * math.pi / BOX_LENGTH
    )


def screen_tile(kx, ky, kz):
    squared = signed(kx) ** 2 + signed(ky) ** 2 + signed(kz) ** 2
    safe = jnp.where(squared > 0, squared, jnp.float32(1.0))
    value = 4.0 * math.pi / safe * (1.0 - jnp.exp(-safe / (4.0 * OMEGA * OMEGA)))
    value = jnp.where(squared > 0, value, jnp.float32(math.pi / (OMEGA * OMEGA)))
    return value * jnp.float32(1.0 / (NG * NG * NG))


def turned(value, by=HALF):
    return pltpu.roll(value, by, 1)


def unpacked(flat, x):
    a, b, c = (flat[pl.ds(x * TILES + k, TURNS, stride=3), :] for k in range(3))
    lane = lax.broadcasted_iota(jnp.int32, a.shape, 1)
    second = jnp.where(lane < 32, turned(a, 32), turned(b, 32))
    third = jnp.where(lane < HALF, turned(b), turned(c))
    return jnp.concatenate([a, second, third, turned(c, 96)], axis=0)


def packed_rows(plane):
    first, second, third, fourth = (plane[k * TURNS : (k + 1) * TURNS] for k in range(TURN))
    lane = lax.broadcasted_iota(jnp.int32, first.shape, 1)
    second, third = turned(second, 96), turned(third)
    return (
        jnp.where(lane < NG, first, second),
        jnp.where(lane < HALF, second, third),
        jnp.where(lane < 32, third, turned(fourth, 32)),
    )


def put(ref, row, value):
    pitch = ref.shape[1]
    ref.reshape(SLABS * pitch, LANES)[pl.ds(row, SLABS, stride=pitch), :] = value


def get(ref, row):
    pitch = ref.shape[1]
    return ref.reshape(SLABS * pitch, LANES)[pl.ds(row, SLABS, stride=pitch), :]


def kernel(
    orbitals, dealt_in, dealt_t_in, to_spectrum_in, from_spectrum_in, out,
    raw, dealt_raw, dealt_t_raw, to_spectrum_raw, from_spectrum_raw,
    dealt, dealt_t, to_spectrum, from_spectrum,
    own_flat, own, partner_flat, partner, to_own,
    sent, arrived, screened, returned, sent_rest, arrived_rest, screened_rest, returned_rest,
    screen, terms, terms_in,
    load_sem, swap_send, swap_recv, send_sem, recv_sem, local_sem,
):
    me = lax.axis_index("grid")
    block = lax.axis_index("blk")
    blocks = lax.axis_size("blk")
    after = lax.rem(block + 1, blocks)
    before = lax.rem(block + blocks - 1, blocks)
    peers = {k: lax.rem(me + k, SLABS) for k in FAR_FIRST}

    barrier = pltpu.get_barrier_semaphore()
    for k in FAR_FIRST:
        pl.semaphore_signal(barrier, inc=1, device_id={"grid": peers[k]}, device_id_type=MESH)
    for neighbour in (before, after):
        pl.semaphore_signal(barrier, inc=1, device_id={"blk": neighbour}, device_id_type=MESH)

    loads = [
        pltpu.make_async_copy(source, target, load_sem.at[k])
        for k, (source, target) in enumerate(
            [
                (orbitals, raw),
                (to_spectrum_in, to_spectrum_raw),
                (dealt_in, dealt_raw),
                (dealt_t_in, dealt_t_raw),
                (from_spectrum_in, from_spectrum_raw),
            ]
        )
    ]
    for load in loads:
        load.start()

    shape = (NG, LANES)
    row = lax.broadcasted_iota(jnp.int32, shape, 0)
    turn = (row >= TURNS).astype(jnp.int32) + (row >= 2 * TURNS) + (row >= 3 * TURNS)
    kx = TURN * (row - TURNS * turn) + turn
    lane = lax.broadcasted_iota(jnp.int32, shape, 1)
    low_half = lane < HALF
    first = PLANES * me
    for r in range(PLANES):
        screen[:, r * LANES : (r + 1) * LANES] = screen_tile(
            kx, jnp.full(shape, first + r, jnp.int32), jnp.where(lane < NG, lane, lane - NG)
        )
    kz = jnp.where(low_half, lane, lane - HALF) + (LANES - NG)
    screen[:, 3 * LANES : 4 * LANES] = screen_tile(kx, jnp.where(low_half, first, first + 1), kz)
    screen[:, 4 * LANES : 5 * LANES] = screen_tile(kx, jnp.full(shape, first + 2, jnp.int32), kz)

    loads[0].wait()
    for i in range(2):
        own_flat[i] = raw[pl.ds(i, PLANES * TILES, stride=2), :]
        for x in range(PLANES):
            own[i, x * NG : (x + 1) * NG] = unpacked(own_flat.at[i], x)
    for load in loads[1:]:
        load.wait()
    for source, target in (
        (to_spectrum_raw, to_spectrum),
        (dealt_raw, dealt),
        (dealt_t_raw, dealt_t),
        (from_spectrum_raw, from_spectrum),
    ):
        target[0], target[1] = halves(source[...])

    pl.semaphore_wait(barrier, SLABS + 1)

    def swap(source, target, slot, whom):
        return pltpu.make_async_remote_copy(
            src_ref=source, dst_ref=target, send_sem=swap_send.at[slot], recv_sem=swap_recv.at[slot],
            device_id={"blk": whom}, device_id_type=MESH,
        )

    orbital_swaps = [swap(own_flat.at[j], partner_flat.at[j], j, after) for j in range(2)]
    for copy in orbital_swaps:
        copy.start()

    def message(source, target, rows, slot, k, origin, peer):
        return pltpu.make_async_remote_copy(
            src_ref=source.at[peer, pl.ds(0, rows)],
            dst_ref=target.at[origin, pl.ds(0, rows)],
            send_sem=send_sem.at[slot, k],
            recv_sem=recv_sem.at[slot, origin],
            device_id={"grid": peer},
            device_id_type=MESH,
        )

    def stay(source, target, rows, slot):
        return pltpu.make_async_copy(source.at[me], target.at[me], local_sem.at[slot])

    def scatter(*job):
        source, target, rows, slot = job
        for k in FAR_FIRST:
            message(*job, k, me, peers[k]).start()
        stay(*job).start()

    def gather(*job):
        for k in FAR_FIRST:
            message(*job, k, peers[k], peers[k]).wait_recv()
        stay(*job).wait()

    def drain(*job):
        for k in FAR_FIRST:
            message(*job, k, me, peers[k]).wait_send()

    out_jobs = [(sent.at[j], arrived.at[j], MAIN, j) for j in range(2)]
    out_rest = (sent_rest, arrived_rest, REST, 2)
    back_jobs = [(screened.at[j], returned.at[j], MAIN, 3 + j) for j in range(2)]
    back_rest = (screened_rest, returned_rest, REST, 5)

    in_low = lax.broadcasted_iota(jnp.int32, (SLABS, LANES), 1) < HALF

    thirds = []
    for j in range(2):
        orbital_swaps[j].wait_recv()
        for x in range(PLANES):
            plane = pl.ds(x * NG, NG)
            other = unpacked(partner_flat.at[j], x)
            partner[j, plane] = other
            density = jnp.concatenate([own[0, plane] * other, own[1, plane] * other], axis=1)
            spectrum = table_times(dealt, times_table(density, to_spectrum))
            rest = []
            for r in range(PLANES):
                rows = spectrum[r * SLABS : (r + 1) * SLABS]
                put(sent.at[j], x * 4 + r, rows[:, :LANES])
                rest.append(rows[:, LANES:])
            put(sent.at[j], x * 4 + 3, jnp.where(in_low, rest[0], rest[1]))
            if j == 0:
                thirds.append(rest[2])
            else:
                put(sent_rest, x, jnp.where(in_low, thirds[x], rest[2]))
        if j == 1:
            scatter(*out_rest)
        scatter(*out_jobs[j])

    def along_x(source, target, width, start):
        columns = []
        for c in range(width):
            columns.append(jnp.concatenate([get(source, x * width + c) for x in range(PLANES)], axis=0))
        spectrum = table_times(dealt_t, jnp.concatenate(columns, axis=1))
        back = table_times(dealt, spectrum * screen[:, start * LANES : (start + width) * LANES])
        for x in range(PLANES):
            rows = back[x * SLABS : (x + 1) * SLABS]
            for c in range(width):
                put(target, x * width + c, rows[:, c * LANES : (c + 1) * LANES])

    gather(*out_jobs[0])
    along_x(arrived.at[0], screened.at[0], 4, 0)
    scatter(*back_jobs[0])
    gather(*out_rest)
    along_x(arrived_rest, screened_rest, 1, 4)
    scatter(*back_rest)
    gather(*out_jobs[1])
    along_x(arrived.at[1], screened.at[1], 4, 0)
    scatter(*back_jobs[1])

    term_swaps = [swap(terms.at[j], terms_in.at[j], 2 + j, before) for j in range(2)]
    gather(*back_rest)
    for j in range(2):
        gather(*back_jobs[j])
        for x in range(PLANES):
            plane = pl.ds(x * NG, NG)
            main = jnp.concatenate([get(returned.at[j], x * 4 + r) for r in range(PLANES)], axis=0)
            both = get(returned.at[j], x * 4 + 3)
            last = get(returned_rest, x)
            if j == 1:
                last = turned(last)
            rest = jnp.concatenate([both, turned(both), last], axis=0)
            potential = times_table(
                table_times(dealt_t, jnp.concatenate([main, rest], axis=1)), from_spectrum
            )
            parts = [potential[:, :LANES], potential[:, LANES:]]
            term = -(parts[0] * own[0, plane] + parts[1] * own[1, plane])
            for k, value in enumerate(packed_rows(term)):
                terms[j, pl.ds(x * TILES + k, TURNS, stride=3), :] = value
            for i in range(2):
                mine = parts[i] * partner[j, plane]
                if j == 0:
                    to_own[i, plane] = -mine
                else:
                    to_own[i, plane] = to_own[i, plane] - mine
        term_swaps[j].start()
    for i in range(2):
        term_swaps[i].wait_recv()
        for x in range(PLANES):
            for k, value in enumerate(packed_rows(to_own[i, pl.ds(x * NG, NG)])):
                theirs = terms_in[i, pl.ds(x * TILES + k, TURNS, stride=3), :]
                out[pl.ds((x * TILES + k) * 2 + i, TURNS, stride=6), :] = value + theirs

    for copy in orbital_swaps + term_swaps:
        copy.wait_send()
    for job in out_jobs + [out_rest] + back_jobs + [back_rest]:
        drain(*job)


def on_device(orbitals):
    count, planes, cells = orbitals.shape
    flat = orbitals.reshape(count, planes, TILES, LANES).transpose(1, 2, 0, 3)
    flat = flat.reshape(planes * TILES * count, LANES)
    vmem = pl.BlockSpec(memory_space=pltpu.VMEM)
    hbm = pl.BlockSpec(memory_space=pltpu.HBM)
    constants = tables()

    def scratch(*shape):
        return pltpu.VMEM(shape, jnp.float32)

    main, rest = scratch(2, SLABS, MAIN_PITCH, LANES), scratch(SLABS, REST_PITCH, LANES)
    as_it_lies, padded = scratch(2, planes * TILES, LANES), scratch(2, planes * NG, LANES)
    terms = pl.pallas_call(
        kernel,
        out_shape=jax.ShapeDtypeStruct(flat.shape, jnp.float32),
        in_specs=[hbm] * 5,
        out_specs=vmem,
        scratch_shapes=[
            scratch(*flat.shape), *(scratch(*t.shape) for t in constants),
            *(pltpu.VMEM((2, *t.shape), jnp.bfloat16) for t in constants),
            as_it_lies, padded, as_it_lies, padded, padded,
            main, main, main, main, rest, rest, rest, rest,
            scratch(NG, 5 * LANES), as_it_lies, as_it_lies,
            pltpu.SemaphoreType.DMA((5,)),
            pltpu.SemaphoreType.DMA((4,)), pltpu.SemaphoreType.DMA((4,)),
            pltpu.SemaphoreType.DMA((6, SLABS)), pltpu.SemaphoreType.DMA((6, SLABS)),
            pltpu.SemaphoreType.DMA((6,)),
        ],
        compiler_params=pltpu.CompilerParams(
            collective_id=0, has_side_effects=True, vmem_limit_bytes=60 * 1024 * 1024
        ),
    )(flat, *constants)
    terms = terms.reshape(planes, TILES, count, LANES).transpose(2, 0, 1, 3)
    return terms.reshape(count, planes, cells)


def solution(mesh):
    spec = P("blk", "grid", None)
    return jax.shard_map(on_device, mesh=mesh, in_specs=(spec,), out_specs=spec, check_vma=False)
```

```python
import math

import jax
import jax.numpy as jnp
import numpy as np
from jax import lax
from jax.experimental import pallas as pl
from jax.experimental.pallas import tpu as pltpu
from jax.sharding import PartitionSpec as P

NG = 96
LANES = 128
HALF = LANES // 2
BOX_LENGTH = 37.25
OMEGA = 0.11
SLABS = 32
PLANES = 3
TILES = NG * NG // LANES
TURN = 4
TURNS = NG // TURN
MAIN = 4 * PLANES
REST = PLANES
MAIN_PITCH = 16
REST_PITCH = 8
MESH = pl.DeviceIdType.MESH
FAR_FIRST = sorted(range(1, SLABS), key=lambda k: abs(k - SLABS // 2))


def tables():
    index = np.arange(NG)
    angle = 2.0 * np.pi / NG * ((index[:, None] * index[None, :]) % NG)
    hartley = np.cos(angle) + np.sin(angle)
    by_slab = (np.arange(PLANES)[:, None] + PLANES * np.arange(SLABS)[None, :]).reshape(-1)
    by_turn = (np.arange(TURN)[:, None] + TURN * np.arange(TURNS)[None, :]).reshape(-1)
    dealt = hartley[by_slab][:, by_turn]
    packed = np.zeros((2 * NG, 2 * LANES))
    for i in range(2):
        packed[i * NG : (i + 1) * NG, i * LANES : i * LANES + NG] = hartley
    to_spectrum = np.concatenate([packed.T, packed.T[:, LANES : 2 * NG]], axis=1)
    from_spectrum = np.concatenate([packed, np.zeros((2 * LANES - 2 * NG, 2 * LANES))], axis=0)
    return tuple(t.astype(np.float32) for t in (dealt, dealt.T, to_spectrum, from_spectrum))


def halves(value):
    high = value.astype(jnp.bfloat16)
    low = (value - high.astype(jnp.float32)).astype(jnp.bfloat16)
    return high, low


def dot(a, b):
    return jnp.dot(a, b, preferred_element_type=jnp.float32)


def times_table(value, table):
    high, low = halves(value)
    return dot(high, table[0]) + (dot(low, table[0]) + dot(high, table[1]))


def table_times(table, value):
    high, low = halves(value)
    return dot(table[0], high) + (dot(table[0], low) + dot(table[1], high))


def signed(index):
    return jnp.where(index < NG - NG // 2, index, index - NG).astype(jnp.float32) * jnp.float32(
        2.0 * math.pi / BOX_LENGTH
    )


def screen_tile(kx, ky, kz):
    squared = signed(kx) ** 2 + signed(ky) ** 2 + signed(kz) ** 2
    safe = jnp.where(squared > 0, squared, jnp.float32(1.0))
    value = 4.0 * math.pi / safe * (1.0 - jnp.exp(-safe / (4.0 * OMEGA * OMEGA)))
    value = jnp.where(squared > 0, value, jnp.float32(math.pi / (OMEGA * OMEGA)))
    return value * jnp.float32(1.0 / (NG * NG * NG))


def turned(value, by=HALF):
    return pltpu.roll(value, by, 1)


def unpacked(flat, x):
    a, b, c = (flat[pl.ds(x * TILES + k, TURNS, stride=3), :] for k in range(3))
    lane = lax.broadcasted_iota(jnp.int32, a.shape, 1)
    second = jnp.where(lane < 32, turned(a, 32), turned(b, 32))
    third = jnp.where(lane < HALF, turned(b), turned(c))
    return jnp.concatenate([a, second, third, turned(c, 96)], axis=0)


def packed_rows(plane):
    first, second, third, fourth = (plane[k * TURNS : (k + 1) * TURNS] for k in range(TURN))
    lane = lax.broadcasted_iota(jnp.int32, first.shape, 1)
    second, third = turned(second, 96), turned(third)
    return (
        jnp.where(lane < NG, first, second),
        jnp.where(lane < HALF, second, third),
        jnp.where(lane < 32, third, turned(fourth, 32)),
    )


def put(ref, row, value):
    pitch = ref.shape[1]
    ref.reshape(SLABS * pitch, LANES)[pl.ds(row, SLABS, stride=pitch), :] = value


def get(ref, row):
    pitch = ref.shape[1]
    return ref.reshape(SLABS * pitch, LANES)[pl.ds(row, SLABS, stride=pitch), :]


def kernel(
    orbitals, dealt_in, dealt_t_in, to_spectrum_in, from_spectrum_in, out,
    raw, dealt_raw, dealt_t_raw, to_spectrum_raw, from_spectrum_raw,
    dealt, dealt_t, to_spectrum, from_spectrum,
    own_flat, own, partner_flat, partner, to_own,
    sent, arrived, screened, returned, screened_rest, returned_rest,
    screen, terms, terms_in,
    load_sem, swap_send, swap_recv, send_sem, recv_sem, local_sem, turn_sem,
):
    me = lax.axis_index("grid")
    block = lax.axis_index("blk")
    blocks = lax.axis_size("blk")
    after = lax.rem(block + 1, blocks)
    before = lax.rem(block + blocks - 1, blocks)
    peers = {k: lax.rem(me + k, SLABS) for k in FAR_FIRST}

    barrier = pltpu.get_barrier_semaphore()
    for k in FAR_FIRST:
        pl.semaphore_signal(barrier, inc=1, device_id={"grid": peers[k]}, device_id_type=MESH)
    for neighbour in (before, after):
        pl.semaphore_signal(barrier, inc=1, device_id={"blk": neighbour}, device_id_type=MESH)

    loads = [
        pltpu.make_async_copy(source, target, load_sem.at[k])
        for k, (source, target) in enumerate(
            [
                (orbitals, raw),
                (to_spectrum_in, to_spectrum_raw),
                (dealt_in, dealt_raw),
                (dealt_t_in, dealt_t_raw),
                (from_spectrum_in, from_spectrum_raw),
            ]
        )
    ]
    for load in loads:
        load.start()

    shape = (NG, LANES)
    row = lax.broadcasted_iota(jnp.int32, shape, 0)
    turn = (row >= TURNS).astype(jnp.int32) + (row >= 2 * TURNS) + (row >= 3 * TURNS)
    kx = TURN * (row - TURNS * turn) + turn
    lane = lax.broadcasted_iota(jnp.int32, shape, 1)
    low_half = lane < HALF
    first = PLANES * me
    for r in range(PLANES):
        screen[:, r * LANES : (r + 1) * LANES] = screen_tile(
            kx, jnp.full(shape, first + r, jnp.int32), jnp.where(lane < NG, lane, lane - NG)
        )
    kz = jnp.where(low_half, lane, lane - HALF) + (LANES - NG)
    screen[:, 3 * LANES : 4 * LANES] = screen_tile(kx, jnp.where(low_half, first, first + 1), kz)
    screen[:, 4 * LANES : 5 * LANES] = screen_tile(kx, jnp.full(shape, first + 2, jnp.int32), kz)

    loads[0].wait()
    for i in range(2):
        own_flat[i] = raw[pl.ds(i, PLANES * TILES, stride=2), :]
        for x in range(PLANES):
            own[i, x * NG : (x + 1) * NG] = unpacked(own_flat.at[i], x)
    for load in loads[1:]:
        load.wait()
    for source, target in (
        (to_spectrum_raw, to_spectrum),
        (dealt_raw, dealt),
        (dealt_t_raw, dealt_t),
        (from_spectrum_raw, from_spectrum),
    ):
        target[0], target[1] = halves(source[...])

    pl.semaphore_wait(barrier, SLABS + 1)

    def swap(source, target, slot, whom):
        return pltpu.make_async_remote_copy(
            src_ref=source, dst_ref=target, send_sem=swap_send.at[slot], recv_sem=swap_recv.at[slot],
            device_id={"blk": whom}, device_id_type=MESH,
        )

    orbital_swaps = [swap(own_flat.at[j], partner_flat.at[j], j, after) for j in range(2)]
    for copy in orbital_swaps:
        copy.start()

    def message(source, target, rows, slot, k, origin, peer):
        return pltpu.make_async_remote_copy(
            src_ref=source.at[peer, pl.ds(0, rows)],
            dst_ref=target.at[origin, pl.ds(0, rows)],
            send_sem=send_sem.at[slot, k],
            recv_sem=recv_sem.at[slot, origin],
            device_id={"grid": peer},
            device_id_type=MESH,
        )

    def stay(source, target, rows, slot):
        return pltpu.make_async_copy(source.at[me], target.at[me], local_sem.at[slot])

    def scatter(*job):
        source, target, rows, slot = job
        for k in FAR_FIRST:
            message(*job, k, me, peers[k]).start()
        stay(*job).start()

    def gather(*job):
        for k in FAR_FIRST:
            message(*job, k, peers[k], peers[k]).wait_recv()
        stay(*job).wait()

    def drain(*job):
        for k in FAR_FIRST:
            message(*job, k, me, peers[k]).wait_send()

    out_jobs = [(sent.at[j], arrived.at[j], MAIN + REST * j, j) for j in range(2)]
    back_jobs = [(screened.at[j], returned.at[j], MAIN, 2 + j) for j in range(2)]
    back_rest = (screened_rest, returned_rest, REST, 4)

    in_low = lax.broadcasted_iota(jnp.int32, (SLABS, LANES), 1) < HALF

    thirds = []
    for j in range(2):
        orbital_swaps[j].wait_recv()
        for x in range(PLANES):
            plane = pl.ds(x * NG, NG)
            other = unpacked(partner_flat.at[j], x)
            partner[j, plane] = other
            density = jnp.concatenate([own[0, plane] * other, own[1, plane] * other], axis=1)
            spectrum = table_times(dealt, times_table(density, to_spectrum))
            rest = []
            for r in range(PLANES):
                rows = spectrum[r * SLABS : (r + 1) * SLABS]
                put(sent.at[j], x * 4 + r, rows[:, :LANES])
                rest.append(rows[:, LANES:])
            put(sent.at[j], x * 4 + 3, jnp.where(in_low, rest[0], rest[1]))
            if j == 0:
                thirds.append(rest[2])
            else:
                put(sent.at[j], MAIN + x, jnp.where(in_low, thirds[x], rest[2]))
        scatter(*out_jobs[j])

    def along_x(source, start, width, tile):
        columns = []
        for c in range(width):
            rows = [get(source, start + x * width + c) for x in range(PLANES)]
            columns.append(jnp.concatenate(rows, axis=0))
        spectrum = table_times(dealt_t, jnp.concatenate(columns, axis=1))
        return table_times(dealt, spectrum * screen[:, tile * LANES : (tile + width) * LANES])

    def deal(target, back, width):
        for x in range(PLANES):
            rows = back[x * SLABS : (x + 1) * SLABS]
            for c in range(width):
                put(target, x * width + c, rows[:, c * LANES : (c + 1) * LANES])

    gather(*out_jobs[0])
    deal(screened.at[0], along_x(arrived.at[0], 0, 4, 0), 4)
    scatter(*back_jobs[0])
    gather(*out_jobs[1])
    deal(screened_rest, along_x(arrived.at[1], MAIN, 1, 4), 1)
    scatter(*back_rest)
    deal(screened.at[1], along_x(arrived.at[1], 0, 4, 0), 4)
    odd = lax.rem(block, 2) == 1

    @pl.when(odd)
    def _():
        pl.semaphore_wait(turn_sem, 1)

    scatter(*back_jobs[1])

    @pl.when(jnp.logical_not(odd))
    def _():
        for k in FAR_FIRST[:24]:
            message(*back_jobs[1], k, me, peers[k]).wait_send()
        pl.semaphore_signal(turn_sem, inc=1, device_id={"blk": after}, device_id_type=MESH)


    term_swaps = [swap(terms.at[j], terms_in.at[j], 2 + j, before) for j in range(2)]
    gather(*back_rest)
    for j in range(2):
        gather(*back_jobs[j])
        for x in range(PLANES):
            plane = pl.ds(x * NG, NG)
            main = jnp.concatenate([get(returned.at[j], x * 4 + r) for r in range(PLANES)], axis=0)
            both = get(returned.at[j], x * 4 + 3)
            last = get(returned_rest, x)
            if j == 1:
                last = turned(last)
            rest = jnp.concatenate([both, turned(both), last], axis=0)
            potential = times_table(
                table_times(dealt_t, jnp.concatenate([main, rest], axis=1)), from_spectrum
            )
            parts = [potential[:, :LANES], potential[:, LANES:]]
            term = -(parts[0] * own[0, plane] + parts[1] * own[1, plane])
            for k, value in enumerate(packed_rows(term)):
                terms[j, pl.ds(x * TILES + k, TURNS, stride=3), :] = value
            for i in range(2):
                mine = parts[i] * partner[j, plane]
                if j == 0:
                    to_own[i, plane] = -mine
                else:
                    to_own[i, plane] = to_own[i, plane] - mine
        term_swaps[j].start()
    for i in range(2):
        term_swaps[i].wait_recv()
        for x in range(PLANES):
            for k, value in enumerate(packed_rows(to_own[i, pl.ds(x * NG, NG)])):
                theirs = terms_in[i, pl.ds(x * TILES + k, TURNS, stride=3), :]
                out[pl.ds((x * TILES + k) * 2 + i, TURNS, stride=6), :] = value + theirs

    for copy in orbital_swaps + term_swaps:
        copy.wait_send()
    for job in [*out_jobs, back_jobs[0], back_rest]:
        drain(*job)
    for k in FAR_FIRST[24:]:
        message(*back_jobs[1], k, me, peers[k]).wait_send()

    @pl.when(odd)
    def _():
        for k in FAR_FIRST[:24]:
            message(*back_jobs[1], k, me, peers[k]).wait_send()


def on_device(orbitals):
    count, planes, cells = orbitals.shape
    flat = orbitals.reshape(count, planes, TILES, LANES).transpose(1, 2, 0, 3)
    flat = flat.reshape(planes * TILES * count, LANES)
    vmem = pl.BlockSpec(memory_space=pltpu.VMEM)
    hbm = pl.BlockSpec(memory_space=pltpu.HBM)
    constants = tables()

    def scratch(*shape):
        return pltpu.VMEM(shape, jnp.float32)

    main, rest = scratch(2, SLABS, MAIN_PITCH, LANES), scratch(SLABS, REST_PITCH, LANES)
    as_it_lies, padded = scratch(2, planes * TILES, LANES), scratch(2, planes * NG, LANES)
    terms = pl.pallas_call(
        kernel,
        out_shape=jax.ShapeDtypeStruct(flat.shape, jnp.float32),
        in_specs=[hbm] * 5,
        out_specs=vmem,
        scratch_shapes=[
            scratch(*flat.shape), *(scratch(*t.shape) for t in constants),
            *(pltpu.VMEM((2, *t.shape), jnp.bfloat16) for t in constants),
            as_it_lies, padded, as_it_lies, padded, padded,
            main, main, main, main, rest, rest,
            scratch(NG, 5 * LANES), as_it_lies, as_it_lies,
            pltpu.SemaphoreType.DMA((5,)),
            pltpu.SemaphoreType.DMA((4,)), pltpu.SemaphoreType.DMA((4,)),
            pltpu.SemaphoreType.DMA((5, SLABS)), pltpu.SemaphoreType.DMA((5, SLABS)),
            pltpu.SemaphoreType.DMA((5,)), pltpu.SemaphoreType.REGULAR,
        ],
        compiler_params=pltpu.CompilerParams(
            collective_id=0, has_side_effects=True, vmem_limit_bytes=60 * 1024 * 1024
        ),
    )(flat, *constants)
    terms = terms.reshape(planes, TILES, count, LANES).transpose(2, 0, 1, 3)
    return terms.reshape(count, planes, cells)


def solution(mesh):
    spec = P("blk", "grid", None)
    return jax.shard_map(on_device, mesh=mesh, in_specs=(spec,), out_specs=spec, check_vma=False)
```

```python
import math

import jax
import jax.numpy as jnp
import numpy as np
from jax import lax
from jax.experimental import pallas as pl
from jax.experimental.pallas import tpu as pltpu
from jax.sharding import PartitionSpec as P

NG = 96
LANES = 128
HALF = LANES // 2
BOX_LENGTH = 37.25
OMEGA = 0.11
SLABS = 32
PLANES = 3
TILES = NG * NG // LANES
TURN = 4
TURNS = NG // TURN
MAIN = 4 * PLANES
REST = PLANES
MAIN_PITCH = 16
REST_PITCH = 8
MESH = pl.DeviceIdType.MESH
FAR_FIRST = sorted(range(1, SLABS), key=lambda k: abs(k - SLABS // 2))


def tables():
    index = np.arange(NG)
    angle = 2.0 * np.pi / NG * ((index[:, None] * index[None, :]) % NG)
    hartley = np.cos(angle) + np.sin(angle)
    by_slab = (np.arange(PLANES)[:, None] + PLANES * np.arange(SLABS)[None, :]).reshape(-1)
    by_turn = (np.arange(TURN)[:, None] + TURN * np.arange(TURNS)[None, :]).reshape(-1)
    dealt = hartley[by_slab][:, by_turn]
    packed = np.zeros((2 * NG, 2 * LANES))
    for i in range(2):
        packed[i * NG : (i + 1) * NG, i * LANES : i * LANES + NG] = hartley
    to_spectrum = np.concatenate([packed.T, packed.T[:, LANES : 2 * NG]], axis=1)
    from_spectrum = np.concatenate([packed, np.zeros((2 * LANES - 2 * NG, 2 * LANES))], axis=0)
    return tuple(t.astype(np.float32) for t in (dealt, dealt.T, to_spectrum, from_spectrum))


def halves(value):
    high = value.astype(jnp.bfloat16)
    low = (value - high.astype(jnp.float32)).astype(jnp.bfloat16)
    return high, low


def dot(a, b):
    return jnp.dot(a, b, preferred_element_type=jnp.float32)


def times_table(value, table):
    high, low = halves(value)
    return dot(high, table[0]) + (dot(low, table[0]) + dot(high, table[1]))


def table_times(table, value):
    high, low = halves(value)
    return dot(table[0], high) + (dot(table[0], low) + dot(table[1], high))


def signed(index):
    return jnp.where(index < NG - NG // 2, index, index - NG).astype(jnp.float32) * jnp.float32(
        2.0 * math.pi / BOX_LENGTH
    )


def screen_tile(kx, ky, kz):
    squared = signed(kx) ** 2 + signed(ky) ** 2 + signed(kz) ** 2
    safe = jnp.where(squared > 0, squared, jnp.float32(1.0))
    value = 4.0 * math.pi / safe * (1.0 - jnp.exp(-safe / (4.0 * OMEGA * OMEGA)))
    value = jnp.where(squared > 0, value, jnp.float32(math.pi / (OMEGA * OMEGA)))
    return value * jnp.float32(1.0 / (NG * NG * NG))


def turned(value, by=HALF):
    return pltpu.roll(value, by, 1)


def unpacked(flat, x):
    a, b, c = (flat[pl.ds(x * TILES + k, TURNS, stride=3), :] for k in range(3))
    lane = lax.broadcasted_iota(jnp.int32, a.shape, 1)
    second = jnp.where(lane < 32, turned(a, 32), turned(b, 32))
    third = jnp.where(lane < HALF, turned(b), turned(c))
    return jnp.concatenate([a, second, third, turned(c, 96)], axis=0)


def packed_rows(plane):
    first, second, third, fourth = (plane[k * TURNS : (k + 1) * TURNS] for k in range(TURN))
    lane = lax.broadcasted_iota(jnp.int32, first.shape, 1)
    second, third = turned(second, 96), turned(third)
    return (
        jnp.where(lane < NG, first, second),
        jnp.where(lane < HALF, second, third),
        jnp.where(lane < 32, third, turned(fourth, 32)),
    )


def put(ref, row, value):
    pitch = ref.shape[1]
    ref.reshape(SLABS * pitch, LANES)[pl.ds(row, SLABS, stride=pitch), :] = value


def get(ref, row):
    pitch = ref.shape[1]
    return ref.reshape(SLABS * pitch, LANES)[pl.ds(row, SLABS, stride=pitch), :]


def kernel(
    orbitals, dealt_in, dealt_t_in, to_spectrum_in, from_spectrum_in, out,
    raw, dealt_raw, dealt_t_raw, to_spectrum_raw, from_spectrum_raw,
    dealt, dealt_t, to_spectrum, from_spectrum,
    own_flat, own, partner_flat, partner, to_own,
    sent, arrived, screened, returned, screened_rest, returned_rest,
    screen, terms, terms_in,
    load_sem, swap_send, swap_recv, send_sem, recv_sem, local_sem, turn_sem,
):
    me = lax.axis_index("grid")
    block = lax.axis_index("blk")
    blocks = lax.axis_size("blk")
    after = lax.rem(block + 1, blocks)
    before = lax.rem(block + blocks - 1, blocks)
    peers = {k: lax.rem(me + k, SLABS) for k in FAR_FIRST}

    barrier = pltpu.get_barrier_semaphore()
    for k in FAR_FIRST:
        pl.semaphore_signal(barrier, inc=1, device_id={"grid": peers[k]}, device_id_type=MESH)
    for neighbour in (before, after):
        pl.semaphore_signal(barrier, inc=1, device_id={"blk": neighbour}, device_id_type=MESH)

    loads = [
        pltpu.make_async_copy(source, target, load_sem.at[k])
        for k, (source, target) in enumerate(
            [
                (orbitals, raw),
                (to_spectrum_in, to_spectrum_raw),
                (dealt_in, dealt_raw),
                (dealt_t_in, dealt_t_raw),
                (from_spectrum_in, from_spectrum_raw),
            ]
        )
    ]
    for load in loads:
        load.start()

    shape = (NG, LANES)
    row = lax.broadcasted_iota(jnp.int32, shape, 0)
    turn = (row >= TURNS).astype(jnp.int32) + (row >= 2 * TURNS) + (row >= 3 * TURNS)
    kx = TURN * (row - TURNS * turn) + turn
    lane = lax.broadcasted_iota(jnp.int32, shape, 1)
    low_half = lane < HALF
    first = PLANES * me
    for r in range(PLANES):
        screen[:, r * LANES : (r + 1) * LANES] = screen_tile(
            kx, jnp.full(shape, first + r, jnp.int32), jnp.where(lane < NG, lane, lane - NG)
        )
    kz = jnp.where(low_half, lane, lane - HALF) + (LANES - NG)
    screen[:, 3 * LANES : 4 * LANES] = screen_tile(kx, jnp.where(low_half, first, first + 1), kz)
    screen[:, 4 * LANES : 5 * LANES] = screen_tile(kx, jnp.full(shape, first + 2, jnp.int32), kz)

    loads[0].wait()
    for i in range(2):
        own_flat[i] = raw[pl.ds(i, PLANES * TILES, stride=2), :]
        for x in range(PLANES):
            own[i, x * NG : (x + 1) * NG] = unpacked(own_flat.at[i], x)
    for load in loads[1:]:
        load.wait()
    for source, target in (
        (to_spectrum_raw, to_spectrum),
        (dealt_raw, dealt),
        (dealt_t_raw, dealt_t),
        (from_spectrum_raw, from_spectrum),
    ):
        target[0], target[1] = halves(source[...])

    pl.semaphore_wait(barrier, SLABS + 1)

    def swap(source, target, slot, whom):
        return pltpu.make_async_remote_copy(
            src_ref=source, dst_ref=target, send_sem=swap_send.at[slot], recv_sem=swap_recv.at[slot],
            device_id={"blk": whom}, device_id_type=MESH,
        )

    orbital_swaps = [swap(own_flat.at[j], partner_flat.at[j], j, after) for j in range(2)]
    for copy in orbital_swaps:
        copy.start()

    def message(source, target, rows, slot, k, origin, peer):
        return pltpu.make_async_remote_copy(
            src_ref=source.at[peer, pl.ds(0, rows)],
            dst_ref=target.at[origin, pl.ds(0, rows)],
            send_sem=send_sem.at[slot, k],
            recv_sem=recv_sem.at[slot, origin],
            device_id={"grid": peer},
            device_id_type=MESH,
        )

    def stay(source, target, rows, slot):
        return pltpu.make_async_copy(source.at[me], target.at[me], local_sem.at[slot])

    def scatter(*job):
        source, target, rows, slot = job
        for k in FAR_FIRST:
            message(*job, k, me, peers[k]).start()
        stay(*job).start()

    def gather(*job):
        for k in FAR_FIRST:
            message(*job, k, peers[k], peers[k]).wait_recv()
        stay(*job).wait()

    def drain(*job):
        for k in FAR_FIRST:
            message(*job, k, me, peers[k]).wait_send()

    out_jobs = [(sent.at[j], arrived.at[j], MAIN + REST * j, j) for j in range(2)]
    back_jobs = [(screened.at[j], returned.at[j], MAIN, 2 + j) for j in range(2)]
    back_rest = (screened_rest, returned_rest, REST, 4)

    in_low = lax.broadcasted_iota(jnp.int32, (SLABS, LANES), 1) < HALF

    thirds = []
    for j in range(2):
        orbital_swaps[j].wait_recv()
        for x in range(PLANES):
            plane = pl.ds(x * NG, NG)
            other = unpacked(partner_flat.at[j], x)
            partner[j, plane] = other
            density = jnp.concatenate([own[0, plane] * other, own[1, plane] * other], axis=1)
            spectrum = table_times(dealt, times_table(density, to_spectrum))
            rest = []
            for r in range(PLANES):
                rows = spectrum[r * SLABS : (r + 1) * SLABS]
                put(sent.at[j], x * 4 + r, rows[:, :LANES])
                rest.append(rows[:, LANES:])
            put(sent.at[j], x * 4 + 3, jnp.where(in_low, rest[0], rest[1]))
            if j == 0:
                thirds.append(rest[2])
            else:
                put(sent.at[j], MAIN + x, jnp.where(in_low, thirds[x], rest[2]))
        scatter(*out_jobs[j])

    def along_x(source, start, width, tile):
        columns = []
        for c in range(width):
            rows = [get(source, start + x * width + c) for x in range(PLANES)]
            columns.append(jnp.concatenate(rows, axis=0))
        spectrum = table_times(dealt_t, jnp.concatenate(columns, axis=1))
        return table_times(dealt, spectrum * screen[:, tile * LANES : (tile + width) * LANES])

    def deal(target, back, width):
        for x in range(PLANES):
            rows = back[x * SLABS : (x + 1) * SLABS]
            for c in range(width):
                put(target, x * width + c, rows[:, c * LANES : (c + 1) * LANES])

    gather(*out_jobs[0])
    deal(screened.at[0], along_x(arrived.at[0], 0, 4, 0), 4)
    scatter(*back_jobs[0])
    gather(*out_jobs[1])
    deal(screened_rest, along_x(arrived.at[1], MAIN, 1, 4), 1)
    scatter(*back_rest)
    deal(screened.at[1], along_x(arrived.at[1], 0, 4, 0), 4)
    odd = lax.rem(block, 2) == 1

    @pl.when(odd)
    def _():
        pl.semaphore_wait(turn_sem, 1)

    scatter(*back_jobs[1])

    @pl.when(jnp.logical_not(odd))
    def _():
        for k in FAR_FIRST[:24]:
            message(*back_jobs[1], k, me, peers[k]).wait_send()
        pl.semaphore_signal(turn_sem, inc=1, device_id={"blk": after}, device_id_type=MESH)


    term_swaps = [swap(terms.at[j], terms_in.at[j], 2 + j, before) for j in range(2)]
    gather(*back_rest)
    for j in range(2):
        gather(*back_jobs[j])
        for x in range(PLANES):
            plane = pl.ds(x * NG, NG)
            main = jnp.concatenate([get(returned.at[j], x * 4 + r) for r in range(PLANES)], axis=0)
            both = get(returned.at[j], x * 4 + 3)
            last = get(returned_rest, x)
            if j == 1:
                last = turned(last)
            rest = jnp.concatenate([both, turned(both), last], axis=0)
            potential = times_table(
                table_times(dealt_t, jnp.concatenate([main, rest], axis=1)), from_spectrum
            )
            parts = [potential[:, :LANES], potential[:, LANES:]]
            term = -(parts[0] * own[0, plane] + parts[1] * own[1, plane])
            for k, value in enumerate(packed_rows(term)):
                terms[j, pl.ds(x * TILES + k, TURNS, stride=3), :] = value
            for i in range(2):
                mine = parts[i] * partner[j, plane]
                if j == 0:
                    to_own[i, plane] = -mine
                else:
                    to_own[i, plane] = to_own[i, plane] - mine
        term_swaps[j].start()
    for i in range(2):
        term_swaps[i].wait_recv()
        for x in range(PLANES):
            for k, value in enumerate(packed_rows(to_own[i, pl.ds(x * NG, NG)])):
                theirs = terms_in[i, pl.ds(x * TILES + k, TURNS, stride=3), :]
                out[pl.ds((x * TILES + k) * 2 + i, TURNS, stride=6), :] = value + theirs

    for copy in orbital_swaps + term_swaps:
        copy.wait_send()
    for job in [*out_jobs, back_jobs[0], back_rest]:
        drain(*job)
    for k in FAR_FIRST[24:]:
        message(*back_jobs[1], k, me, peers[k]).wait_send()

    @pl.when(odd)
    def _():
        for k in FAR_FIRST[:24]:
            message(*back_jobs[1], k, me, peers[k]).wait_send()


def on_device(orbitals):
    count, planes, cells = orbitals.shape
    flat = orbitals.reshape(count, planes, TILES, LANES).transpose(1, 2, 0, 3)
    flat = flat.reshape(planes * TILES * count, LANES)
    vmem = pl.BlockSpec(memory_space=pltpu.VMEM)
    hbm = pl.BlockSpec(memory_space=pltpu.HBM)
    constants = tables()

    def scratch(*shape):
        return pltpu.VMEM(shape, jnp.float32)

    main, rest = scratch(2, SLABS, MAIN_PITCH, LANES), scratch(SLABS, REST_PITCH, LANES)
    as_it_lies, padded = scratch(2, planes * TILES, LANES), scratch(2, planes * NG, LANES)
    terms = pl.pallas_call(
        kernel,
        out_shape=jax.ShapeDtypeStruct(flat.shape, jnp.float32),
        in_specs=[hbm] * 5,
        out_specs=vmem,
        scratch_shapes=[
            scratch(*flat.shape), *(scratch(*t.shape) for t in constants),
            *(pltpu.VMEM((2, *t.shape), jnp.bfloat16) for t in constants),
            as_it_lies, padded, as_it_lies, padded, padded,
            main, main, main, main, rest, rest,
            scratch(NG, 5 * LANES), as_it_lies, as_it_lies,
            pltpu.SemaphoreType.DMA((5,)),
            pltpu.SemaphoreType.DMA((4,)), pltpu.SemaphoreType.DMA((4,)),
            pltpu.SemaphoreType.DMA((5, SLABS)), pltpu.SemaphoreType.DMA((5, SLABS)),
            pltpu.SemaphoreType.DMA((5,)), pltpu.SemaphoreType.REGULAR,
        ],
        compiler_params=pltpu.CompilerParams(
            collective_id=0, has_side_effects=True, vmem_limit_bytes=32 * 1024 * 1024
        ),
    )(*(pltpu.with_memory_space_constraint(a, pltpu.HBM) for a in (flat, *map(jnp.asarray, constants))))
    terms = terms.reshape(planes, TILES, count, LANES).transpose(2, 0, 1, 3)
    return terms.reshape(count, planes, cells)


def solution(mesh):
    spec = P("blk", "grid", None)
    return jax.shard_map(on_device, mesh=mesh, in_specs=(spec,), out_specs=spec, check_vma=False)
```

```python
import math

import jax
import jax.numpy as jnp
import numpy as np
from jax import lax
from jax.experimental import pallas as pl
from jax.experimental.pallas import tpu as pltpu
from jax.sharding import PartitionSpec as P

NG = 96
LANES = 128
HALF = LANES // 2
BOX_LENGTH = 37.25
OMEGA = 0.11
SLABS = 32
PLANES = 3
TILES = NG * NG // LANES
TURN = 4
TURNS = NG // TURN
MAIN = 4 * PLANES
REST = PLANES
MAIN_PITCH = 16
REST_PITCH = 8
MESH = pl.DeviceIdType.MESH
FAR_FIRST = sorted(range(1, SLABS), key=lambda k: abs(k - SLABS // 2))


def tables():
    index = np.arange(NG)
    angle = 2.0 * np.pi / NG * ((index[:, None] * index[None, :]) % NG)
    hartley = np.cos(angle) + np.sin(angle)
    by_slab = (np.arange(PLANES)[:, None] + PLANES * np.arange(SLABS)[None, :]).reshape(-1)
    by_turn = (np.arange(TURN)[:, None] + TURN * np.arange(TURNS)[None, :]).reshape(-1)
    dealt = hartley[by_slab][:, by_turn]
    packed = np.zeros((2 * NG, 2 * LANES))
    for i in range(2):
        packed[i * NG : (i + 1) * NG, i * LANES : i * LANES + NG] = hartley
    to_spectrum = np.concatenate([packed.T, packed.T[:, LANES : 2 * NG]], axis=1)
    from_spectrum = np.concatenate([packed, np.zeros((2 * LANES - 2 * NG, 2 * LANES))], axis=0)
    return tuple(t.astype(np.float32) for t in (dealt, dealt.T, to_spectrum, from_spectrum))


def halves(value):
    high = value.astype(jnp.bfloat16)
    low = (value - high.astype(jnp.float32)).astype(jnp.bfloat16)
    return high, low


def dot(a, b):
    return jnp.dot(a, b, preferred_element_type=jnp.float32)


def times_table(value, table):
    high, low = halves(value)
    return dot(high, table[0]) + (dot(low, table[0]) + dot(high, table[1]))


def table_times(table, value):
    high, low = halves(value)
    return dot(table[0], high) + (dot(table[0], low) + dot(table[1], high))


def signed(index):
    return jnp.where(index < NG - NG // 2, index, index - NG).astype(jnp.float32) * jnp.float32(
        2.0 * math.pi / BOX_LENGTH
    )


def screen_tile(kx, ky, kz):
    squared = signed(kx) ** 2 + signed(ky) ** 2 + signed(kz) ** 2
    safe = jnp.where(squared > 0, squared, jnp.float32(1.0))
    value = 4.0 * math.pi / safe * (1.0 - jnp.exp(-safe / (4.0 * OMEGA * OMEGA)))
    value = jnp.where(squared > 0, value, jnp.float32(math.pi / (OMEGA * OMEGA)))
    return value * jnp.float32(1.0 / (NG * NG * NG))


def turned(value, by=HALF):
    return pltpu.roll(value, by, 1)


def unpacked(flat, x):
    a, b, c = (flat[pl.ds(x * TILES + k, TURNS, stride=3), :] for k in range(3))
    lane = lax.broadcasted_iota(jnp.int32, a.shape, 1)
    second = jnp.where(lane < 32, turned(a, 32), turned(b, 32))
    third = jnp.where(lane < HALF, turned(b), turned(c))
    return jnp.concatenate([a, second, third, turned(c, 96)], axis=0)


def packed_rows(plane):
    first, second, third, fourth = (plane[k * TURNS : (k + 1) * TURNS] for k in range(TURN))
    lane = lax.broadcasted_iota(jnp.int32, first.shape, 1)
    second, third = turned(second, 96), turned(third)
    return (
        jnp.where(lane < NG, first, second),
        jnp.where(lane < HALF, second, third),
        jnp.where(lane < 32, third, turned(fourth, 32)),
    )


def put(ref, row, value):
    pitch = ref.shape[1]
    ref.reshape(SLABS * pitch, LANES)[pl.ds(row, SLABS, stride=pitch), :] = value


def get(ref, row):
    pitch = ref.shape[1]
    return ref.reshape(SLABS * pitch, LANES)[pl.ds(row, SLABS, stride=pitch), :]


def kernel(
    orbitals, dealt_in, dealt_t_in, to_spectrum_in, from_spectrum_in, out,
    raw, dealt_raw, dealt_t_raw, to_spectrum_raw, from_spectrum_raw,
    dealt, dealt_t, to_spectrum, from_spectrum,
    own_flat, own, partner_flat, partner, to_own,
    sent, arrived, screened, returned, screened_rest, returned_rest,
    screen, terms, terms_in,
    load_sem, swap_send, swap_recv, send_sem, recv_sem, local_sem, turn_sem,
):
    me = lax.axis_index("grid")
    block = lax.axis_index("blk")
    blocks = lax.axis_size("blk")
    after = lax.rem(block + 1, blocks)
    before = lax.rem(block + blocks - 1, blocks)
    peers = {k: lax.rem(me + k, SLABS) for k in FAR_FIRST}

    barrier = pltpu.get_barrier_semaphore()
    for k in FAR_FIRST:
        pl.semaphore_signal(barrier, inc=1, device_id={"grid": peers[k]}, device_id_type=MESH)
    for neighbour in (before, after):
        pl.semaphore_signal(barrier, inc=1, device_id={"blk": neighbour}, device_id_type=MESH)

    loads = [
        pltpu.make_async_copy(source, target, load_sem.at[k])
        for k, (source, target) in enumerate(
            [
                (orbitals, raw),
                (to_spectrum_in, to_spectrum_raw),
                (dealt_in, dealt_raw),
                (dealt_t_in, dealt_t_raw),
                (from_spectrum_in, from_spectrum_raw),
            ]
        )
    ]
    for load in loads:
        load.start()

    shape = (NG, LANES)
    row = lax.broadcasted_iota(jnp.int32, shape, 0)
    turn = (row >= TURNS).astype(jnp.int32) + (row >= 2 * TURNS) + (row >= 3 * TURNS)
    kx = TURN * (row - TURNS * turn) + turn
    lane = lax.broadcasted_iota(jnp.int32, shape, 1)
    low_half = lane < HALF
    first = PLANES * me
    for r in range(PLANES):
        screen[:, r * LANES : (r + 1) * LANES] = screen_tile(
            kx, jnp.full(shape, first + r, jnp.int32), jnp.where(lane < NG, lane, lane - NG)
        )
    kz = jnp.where(low_half, lane, lane - HALF) + (LANES - NG)
    screen[:, 3 * LANES : 4 * LANES] = screen_tile(kx, jnp.where(low_half, first, first + 1), kz)
    screen[:, 4 * LANES : 5 * LANES] = screen_tile(kx, jnp.full(shape, first + 2, jnp.int32), kz)

    loads[0].wait()
    for i in range(2):
        own_flat[i] = raw[pl.ds(i, PLANES * TILES, stride=2), :]
        for x in range(PLANES):
            own[i, x * NG : (x + 1) * NG] = unpacked(own_flat.at[i], x)
    for load in loads[1:]:
        load.wait()
    for source, target in (
        (to_spectrum_raw, to_spectrum),
        (dealt_raw, dealt),
        (dealt_t_raw, dealt_t),
        (from_spectrum_raw, from_spectrum),
    ):
        target[0], target[1] = halves(source[...])

    pl.semaphore_wait(barrier, SLABS + 1)

    def swap(source, target, slot, whom):
        return pltpu.make_async_remote_copy(
            src_ref=source, dst_ref=target, send_sem=swap_send.at[slot], recv_sem=swap_recv.at[slot],
            device_id={"blk": whom}, device_id_type=MESH,
        )

    orbital_swaps = [swap(own_flat.at[j], partner_flat.at[j], j, after) for j in range(2)]
    for copy in orbital_swaps:
        copy.start()

    def message(source, target, rows, slot, k, origin, peer):
        return pltpu.make_async_remote_copy(
            src_ref=source.at[peer, pl.ds(0, rows)],
            dst_ref=target.at[origin, pl.ds(0, rows)],
            send_sem=send_sem.at[slot, k],
            recv_sem=recv_sem.at[slot, origin],
            device_id={"grid": peer},
            device_id_type=MESH,
        )

    def stay(source, target, rows, slot):
        return pltpu.make_async_copy(source.at[me], target.at[me], local_sem.at[slot])

    def scatter(*job):
        source, target, rows, slot = job
        for k in FAR_FIRST:
            message(*job, k, me, peers[k]).start()
        stay(*job).start()

    def gather(*job):
        for k in FAR_FIRST:
            message(*job, k, peers[k], peers[k]).wait_recv()
        stay(*job).wait()

    def drain(*job):
        for k in FAR_FIRST:
            message(*job, k, me, peers[k]).wait_send()

    out_jobs = [(sent.at[j], arrived.at[j], MAIN + REST * j, j) for j in range(2)]
    back_jobs = [(screened.at[j], returned.at[j], MAIN, 2 + j) for j in range(2)]
    back_rest = (screened_rest, returned_rest, REST, 4)

    in_low = lax.broadcasted_iota(jnp.int32, (SLABS, LANES), 1) < HALF

    thirds = []
    for j in range(2):
        orbital_swaps[j].wait_recv()
        for x in range(PLANES):
            plane = pl.ds(x * NG, NG)
            other = unpacked(partner_flat.at[j], x)
            partner[j, plane] = other
            density = jnp.concatenate([own[0, plane] * other, own[1, plane] * other], axis=1)
            spectrum = table_times(dealt, times_table(density, to_spectrum))
            rest = []
            for r in range(PLANES):
                rows = spectrum[r * SLABS : (r + 1) * SLABS]
                put(sent.at[j], x * 4 + r, rows[:, :LANES])
                rest.append(rows[:, LANES:])
            put(sent.at[j], x * 4 + 3, jnp.where(in_low, rest[0], rest[1]))
            if j == 0:
                thirds.append(rest[2])
            else:
                put(sent.at[j], MAIN + x, jnp.where(in_low, thirds[x], rest[2]))
        scatter(*out_jobs[j])

    def along_x(source, start, width, tile):
        columns = []
        for c in range(width):
            rows = [get(source, start + x * width + c) for x in range(PLANES)]
            columns.append(jnp.concatenate(rows, axis=0))
        spectrum = table_times(dealt_t, jnp.concatenate(columns, axis=1))
        return table_times(dealt, spectrum * screen[:, tile * LANES : (tile + width) * LANES])

    def deal(target, back, width):
        for x in range(PLANES):
            rows = back[x * SLABS : (x + 1) * SLABS]
            for c in range(width):
                put(target, x * width + c, rows[:, c * LANES : (c + 1) * LANES])

    gather(*out_jobs[0])
    deal(screened.at[0], along_x(arrived.at[0], 0, 4, 0), 4)
    scatter(*back_jobs[0])
    gather(*out_jobs[1])
    deal(screened_rest, along_x(arrived.at[1], MAIN, 1, 4), 1)
    scatter(*back_rest)
    deal(screened.at[1], along_x(arrived.at[1], 0, 4, 0), 4)
    odd = lax.rem(block, 2) == 1

    @pl.when(odd)
    def _():
        pl.semaphore_wait(turn_sem, 1)

    scatter(*back_jobs[1])

    @pl.when(jnp.logical_not(odd))
    def _():
        for k in FAR_FIRST[:24]:
            message(*back_jobs[1], k, me, peers[k]).wait_send()
        pl.semaphore_signal(turn_sem, inc=1, device_id={"blk": after}, device_id_type=MESH)

    for copy in orbital_swaps:
        copy.wait_send()
    for job in out_jobs:
        drain(*job)

    term_swaps = [swap(terms.at[j], terms_in.at[j], 2 + j, before) for j in range(2)]
    gather(*back_rest)
    for j in range(2):
        gather(*back_jobs[j])
        for x in range(PLANES):
            plane = pl.ds(x * NG, NG)
            main = jnp.concatenate([get(returned.at[j], x * 4 + r) for r in range(PLANES)], axis=0)
            both = get(returned.at[j], x * 4 + 3)
            last = get(returned_rest, x)
            if j == 1:
                last = turned(last)
            rest = jnp.concatenate([both, turned(both), last], axis=0)
            potential = times_table(
                table_times(dealt_t, jnp.concatenate([main, rest], axis=1)), from_spectrum
            )
            parts = [potential[:, :LANES], potential[:, LANES:]]
            term = -(parts[0] * own[0, plane] + parts[1] * own[1, plane])
            for k, value in enumerate(packed_rows(term)):
                terms[j, pl.ds(x * TILES + k, TURNS, stride=3), :] = value
            for i in range(2):
                mine = parts[i] * partner[j, plane]
                if j == 0:
                    to_own[i, plane] = -mine
                else:
                    to_own[i, plane] = to_own[i, plane] - mine
        term_swaps[j].start()
        if j == 0:
            drain(*back_jobs[0])
            drain(*back_rest)
    for k in FAR_FIRST[24:]:
        message(*back_jobs[1], k, me, peers[k]).wait_send()

    @pl.when(odd)
    def _():
        for k in FAR_FIRST[:24]:
            message(*back_jobs[1], k, me, peers[k]).wait_send()

    for i in range(2):
        term_swaps[i].wait_recv()
        for x in range(PLANES):
            for k, value in enumerate(packed_rows(to_own[i, pl.ds(x * NG, NG)])):
                theirs = terms_in[i, pl.ds(x * TILES + k, TURNS, stride=3), :]
                out[pl.ds((x * TILES + k) * 2 + i, TURNS, stride=6), :] = value + theirs

    for copy in term_swaps:
        copy.wait_send()


def on_device(orbitals):
    count, planes, cells = orbitals.shape
    flat = orbitals.reshape(count, planes, TILES, LANES).transpose(1, 2, 0, 3)
    flat = flat.reshape(planes * TILES * count, LANES)
    vmem = pl.BlockSpec(memory_space=pltpu.VMEM)
    hbm = pl.BlockSpec(memory_space=pltpu.HBM)
    constants = tables()

    def scratch(*shape):
        return pltpu.VMEM(shape, jnp.float32)

    main, rest = scratch(2, SLABS, MAIN_PITCH, LANES), scratch(SLABS, REST_PITCH, LANES)
    as_it_lies, padded = scratch(2, planes * TILES, LANES), scratch(2, planes * NG, LANES)
    terms = pl.pallas_call(
        kernel,
        out_shape=jax.ShapeDtypeStruct(flat.shape, jnp.float32),
        in_specs=[hbm] * 5,
        out_specs=vmem,
        scratch_shapes=[
            scratch(*flat.shape), *(scratch(*t.shape) for t in constants),
            *(pltpu.VMEM((2, *t.shape), jnp.bfloat16) for t in constants),
            as_it_lies, padded, as_it_lies, padded, padded,
            main, main, main, main, rest, rest,
            scratch(NG, 5 * LANES), as_it_lies, as_it_lies,
            pltpu.SemaphoreType.DMA((5,)),
            pltpu.SemaphoreType.DMA((4,)), pltpu.SemaphoreType.DMA((4,)),
            pltpu.SemaphoreType.DMA((5, SLABS)), pltpu.SemaphoreType.DMA((5, SLABS)),
            pltpu.SemaphoreType.DMA((5,)), pltpu.SemaphoreType.REGULAR,
        ],
        compiler_params=pltpu.CompilerParams(
            collective_id=0, has_side_effects=True, vmem_limit_bytes=32 * 1024 * 1024
        ),
    )(*(pltpu.with_memory_space_constraint(a, pltpu.HBM) for a in (flat, *map(jnp.asarray, constants))))
    terms = terms.reshape(planes, TILES, count, LANES).transpose(2, 0, 1, 3)
    return terms.reshape(count, planes, cells)


def solution(mesh):
    spec = P("blk", "grid", None)
    return jax.shard_map(on_device, mesh=mesh, in_specs=(spec,), out_specs=spec, check_vma=False)
```

```python
import math

import jax
import jax.numpy as jnp
import numpy as np
from jax import lax
from jax.experimental import pallas as pl
from jax.experimental.pallas import tpu as pltpu
from jax.sharding import PartitionSpec as P

NG = 96
LANES = 128
HALF = LANES // 2
BOX_LENGTH = 37.25
OMEGA = 0.11
SLABS = 32
PLANES = 3
TILES = NG * NG // LANES
TURN = 4
TURNS = NG // TURN
MAIN = 4 * PLANES
REST = PLANES
MAIN_PITCH = 16
REST_PITCH = 8
MESH = pl.DeviceIdType.MESH
FAR_FIRST = sorted(range(1, SLABS), key=lambda k: abs(k - SLABS // 2))


def tables():
    index = np.arange(NG)
    angle = 2.0 * np.pi / NG * ((index[:, None] * index[None, :]) % NG)
    hartley = np.cos(angle) + np.sin(angle)
    by_slab = (np.arange(PLANES)[:, None] + PLANES * np.arange(SLABS)[None, :]).reshape(-1)
    by_turn = (np.arange(TURN)[:, None] + TURN * np.arange(TURNS)[None, :]).reshape(-1)
    dealt = hartley[by_slab][:, by_turn]
    packed = np.zeros((2 * NG, 2 * LANES))
    for i in range(2):
        packed[i * NG : (i + 1) * NG, i * LANES : i * LANES + NG] = hartley
    to_spectrum = np.concatenate([packed.T, packed.T[:, LANES : 2 * NG]], axis=1)
    from_spectrum = np.concatenate([packed, np.zeros((2 * LANES - 2 * NG, 2 * LANES))], axis=0)
    return tuple(t.astype(np.float32) for t in (dealt, dealt.T, to_spectrum, from_spectrum))


def halves(value):
    high = value.astype(jnp.bfloat16)
    low = (value - high.astype(jnp.float32)).astype(jnp.bfloat16)
    return high, low


def dot(a, b):
    return jnp.dot(a, b, preferred_element_type=jnp.float32)


def times_table(value, table):
    high, low = halves(value)
    return dot(high, table[0]) + (dot(low, table[0]) + dot(high, table[1]))


def table_times(table, value):
    high, low = halves(value)
    return dot(table[0], high) + (dot(table[0], low) + dot(table[1], high))


def signed(index):
    return jnp.where(index < NG - NG // 2, index, index - NG).astype(jnp.float32) * jnp.float32(
        2.0 * math.pi / BOX_LENGTH
    )


def screen_tile(kx, ky, kz):
    squared = signed(kx) ** 2 + signed(ky) ** 2 + signed(kz) ** 2
    safe = jnp.where(squared > 0, squared, jnp.float32(1.0))
    value = 4.0 * math.pi / safe * (1.0 - jnp.exp(-safe / (4.0 * OMEGA * OMEGA)))
    value = jnp.where(squared > 0, value, jnp.float32(math.pi / (OMEGA * OMEGA)))
    return value * jnp.float32(1.0 / (NG * NG * NG))


def turned(value, by=HALF):
    return pltpu.roll(value, by, 1)


def unpacked(flat, x):
    a, b, c = (flat[pl.ds(x * TILES + k, TURNS, stride=3), :] for k in range(3))
    lane = lax.broadcasted_iota(jnp.int32, a.shape, 1)
    second = jnp.where(lane < 32, turned(a, 32), turned(b, 32))
    third = jnp.where(lane < HALF, turned(b), turned(c))
    return jnp.concatenate([a, second, third, turned(c, 96)], axis=0)


def packed_rows(plane):
    first, second, third, fourth = (plane[k * TURNS : (k + 1) * TURNS] for k in range(TURN))
    lane = lax.broadcasted_iota(jnp.int32, first.shape, 1)
    second, third = turned(second, 96), turned(third)
    return (
        jnp.where(lane < NG, first, second),
        jnp.where(lane < HALF, second, third),
        jnp.where(lane < 32, third, turned(fourth, 32)),
    )


def put(ref, row, value):
    pitch = ref.shape[1]
    ref.reshape(SLABS * pitch, LANES)[pl.ds(row, SLABS, stride=pitch), :] = value


def get(ref, row):
    pitch = ref.shape[1]
    return ref.reshape(SLABS * pitch, LANES)[pl.ds(row, SLABS, stride=pitch), :]


def kernel(
    orbitals, dealt_in, dealt_t_in, to_spectrum_in, from_spectrum_in, out,
    raw, dealt_raw, dealt_t_raw, to_spectrum_raw, from_spectrum_raw,
    dealt, dealt_t, to_spectrum, from_spectrum,
    own_flat, own, partner_flat, partner, to_own,
    sent, arrived, screened, returned, screened_rest, returned_rest,
    screen, terms, terms_in,
    load_sem, swap_send, swap_recv, send_sem, recv_sem, local_sem, turn_sem,
):
    me = lax.axis_index("grid")
    block = lax.axis_index("blk")
    blocks = lax.axis_size("blk")
    after = lax.rem(block + 1, blocks)
    before = lax.rem(block + blocks - 1, blocks)
    peers = {k: lax.rem(me + k, SLABS) for k in FAR_FIRST}

    barrier = pltpu.get_barrier_semaphore()
    for k in FAR_FIRST:
        pl.semaphore_signal(barrier, inc=1, device_id={"grid": peers[k]}, device_id_type=MESH)
    for neighbour in (before, after):
        pl.semaphore_signal(barrier, inc=1, device_id={"blk": neighbour}, device_id_type=MESH)

    loads = [
        pltpu.make_async_copy(source, target, load_sem.at[k])
        for k, (source, target) in enumerate(
            [
                (orbitals, raw),
                (to_spectrum_in, to_spectrum_raw),
                (dealt_in, dealt_raw),
                (dealt_t_in, dealt_t_raw),
                (from_spectrum_in, from_spectrum_raw),
            ]
        )
    ]
    for load in loads:
        load.start()

    shape = (NG, LANES)
    row = lax.broadcasted_iota(jnp.int32, shape, 0)
    turn = (row >= TURNS).astype(jnp.int32) + (row >= 2 * TURNS) + (row >= 3 * TURNS)
    kx = TURN * (row - TURNS * turn) + turn
    lane = lax.broadcasted_iota(jnp.int32, shape, 1)
    low_half = lane < HALF
    first = PLANES * me
    for r in range(PLANES):
        screen[:, r * LANES : (r + 1) * LANES] = screen_tile(
            kx, jnp.full(shape, first + r, jnp.int32), jnp.where(lane < NG, lane, lane - NG)
        )
    kz = jnp.where(low_half, lane, lane - HALF) + (LANES - NG)
    screen[:, 3 * LANES : 4 * LANES] = screen_tile(kx, jnp.where(low_half, first, first + 1), kz)
    screen[:, 4 * LANES : 5 * LANES] = screen_tile(kx, jnp.full(shape, first + 2, jnp.int32), kz)

    loads[0].wait()
    for i in range(2):
        own_flat[i] = raw[pl.ds(i, PLANES * TILES, stride=2), :]
        for x in range(PLANES):
            own[i, x * NG : (x + 1) * NG] = unpacked(own_flat.at[i], x)
    for load in loads[1:]:
        load.wait()
    for source, target in (
        (to_spectrum_raw, to_spectrum),
        (dealt_raw, dealt),
        (dealt_t_raw, dealt_t),
        (from_spectrum_raw, from_spectrum),
    ):
        target[0], target[1] = halves(source[...])

    pl.semaphore_wait(barrier, SLABS + 1)

    def swap(source, target, slot, whom):
        return pltpu.make_async_remote_copy(
            src_ref=source, dst_ref=target, send_sem=swap_send.at[slot], recv_sem=swap_recv.at[slot],
            device_id={"blk": whom}, device_id_type=MESH,
        )

    orbital_swaps = [swap(own_flat.at[j], partner_flat.at[j], j, after) for j in range(2)]
    for copy in orbital_swaps:
        copy.start()

    def message(source, target, rows, slot, k, origin, peer):
        return pltpu.make_async_remote_copy(
            src_ref=source.at[peer, pl.ds(0, rows)],
            dst_ref=target.at[origin, pl.ds(0, rows)],
            send_sem=send_sem.at[slot, k],
            recv_sem=recv_sem.at[slot, origin],
            device_id={"grid": peer},
            device_id_type=MESH,
        )

    def stay(source, target, rows, slot):
        return pltpu.make_async_copy(source.at[me], target.at[me], local_sem.at[slot])

    def scatter(*job):
        source, target, rows, slot = job
        for k in FAR_FIRST:
            message(*job, k, me, peers[k]).start()
        stay(*job).start()

    def gather(*job):
        for k in FAR_FIRST:
            message(*job, k, peers[k], peers[k]).wait_recv()
        stay(*job).wait()

    def drain(*job):
        for k in FAR_FIRST:
            message(*job, k, me, peers[k]).wait_send()

    out_jobs = [(sent.at[j], arrived.at[j], MAIN + REST * j, j) for j in range(2)]
    back_jobs = [(screened.at[j], returned.at[j], MAIN, 2 + j) for j in range(2)]
    back_rest = (screened_rest, returned_rest, REST, 4)

    in_low = lax.broadcasted_iota(jnp.int32, (SLABS, LANES), 1) < HALF

    thirds = []
    for j in range(2):
        orbital_swaps[j].wait_recv()
        for x in range(PLANES):
            plane = pl.ds(x * NG, NG)
            other = unpacked(partner_flat.at[j], x)
            partner[j, plane] = other
            density = jnp.concatenate([own[0, plane] * other, own[1, plane] * other], axis=1)
            spectrum = table_times(dealt, times_table(density, to_spectrum))
            rest = []
            for r in range(PLANES):
                rows = spectrum[r * SLABS : (r + 1) * SLABS]
                put(sent.at[j], x * 4 + r, rows[:, :LANES])
                rest.append(rows[:, LANES:])
            put(sent.at[j], x * 4 + 3, jnp.where(in_low, rest[0], rest[1]))
            if j == 0:
                thirds.append(rest[2])
            else:
                put(sent.at[j], MAIN + x, jnp.where(in_low, thirds[x], rest[2]))
        scatter(*out_jobs[j])

    def along_x(source, start, width, tile):
        columns = []
        for c in range(width):
            rows = [get(source, start + x * width + c) for x in range(PLANES)]
            columns.append(jnp.concatenate(rows, axis=0))
        spectrum = table_times(dealt_t, jnp.concatenate(columns, axis=1))
        return table_times(dealt, spectrum * screen[:, tile * LANES : (tile + width) * LANES])

    def deal(target, back, width):
        for x in range(PLANES):
            rows = back[x * SLABS : (x + 1) * SLABS]
            for c in range(width):
                put(target, x * width + c, rows[:, c * LANES : (c + 1) * LANES])

    gather(*out_jobs[0])
    deal(screened.at[0], along_x(arrived.at[0], 0, 4, 0), 4)
    scatter(*back_jobs[0])
    gather(*out_jobs[1])
    deal(screened_rest, along_x(arrived.at[1], MAIN, 1, 4), 1)
    scatter(*back_rest)
    deal(screened.at[1], along_x(arrived.at[1], 0, 4, 0), 4)
    odd = lax.rem(block, 2) == 1

    @pl.when(odd)
    def _():
        pl.semaphore_wait(turn_sem, 1)

    scatter(*back_jobs[1])

    @pl.when(jnp.logical_not(odd))
    def _():
        for k in FAR_FIRST[:24]:
            message(*back_jobs[1], k, me, peers[k]).wait_send()
        pl.semaphore_signal(turn_sem, inc=1, device_id={"blk": after}, device_id_type=MESH)

    for copy in orbital_swaps:
        copy.wait_send()
    for job in out_jobs:
        drain(*job)

    term_swaps = [swap(terms.at[j], terms_in.at[j], 2 + j, before) for j in range(2)]
    gather(*back_rest)
    for j in range(2):
        gather(*back_jobs[j])
        planes = []
        for x in range(PLANES):
            plane = pl.ds(x * NG, NG)
            main = jnp.concatenate([get(returned.at[j], x * 4 + r) for r in range(PLANES)], axis=0)
            both = get(returned.at[j], x * 4 + 3)
            last = get(returned_rest, x)
            if j == 1:
                last = turned(last)
            rest = jnp.concatenate([both, turned(both), last], axis=0)
            potential = times_table(
                table_times(dealt_t, jnp.concatenate([main, rest], axis=1)), from_spectrum
            )
            parts = [potential[:, :LANES], potential[:, LANES:]]
            planes.append(parts)
            term = -(parts[0] * own[0, plane] + parts[1] * own[1, plane])
            for k, value in enumerate(packed_rows(term)):
                terms[j, pl.ds(x * TILES + k, TURNS, stride=3), :] = value
        term_swaps[j].start()
        for x in range(PLANES):
            plane = pl.ds(x * NG, NG)
            for i in range(2):
                mine = planes[x][i] * partner[j, plane]
                if j == 0:
                    to_own[i, plane] = -mine
                else:
                    to_own[i, plane] = to_own[i, plane] - mine
        if j == 0:
            drain(*back_jobs[0])
            drain(*back_rest)
    for k in FAR_FIRST[24:]:
        message(*back_jobs[1], k, me, peers[k]).wait_send()

    @pl.when(odd)
    def _():
        for k in FAR_FIRST[:24]:
            message(*back_jobs[1], k, me, peers[k]).wait_send()

    for i in range(2):
        term_swaps[i].wait_recv()
        for x in range(PLANES):
            for k, value in enumerate(packed_rows(to_own[i, pl.ds(x * NG, NG)])):
                theirs = terms_in[i, pl.ds(x * TILES + k, TURNS, stride=3), :]
                out[pl.ds((x * TILES + k) * 2 + i, TURNS, stride=6), :] = value + theirs

    for copy in term_swaps:
        copy.wait_send()


def on_device(orbitals):
    count, planes, cells = orbitals.shape
    flat = orbitals.reshape(count, planes, TILES, LANES).transpose(1, 2, 0, 3)
    flat = flat.reshape(planes * TILES * count, LANES)
    vmem = pl.BlockSpec(memory_space=pltpu.VMEM)
    hbm = pl.BlockSpec(memory_space=pltpu.HBM)
    constants = tables()

    def scratch(*shape):
        return pltpu.VMEM(shape, jnp.float32)

    main, rest = scratch(2, SLABS, MAIN_PITCH, LANES), scratch(SLABS, REST_PITCH, LANES)
    as_it_lies, padded = scratch(2, planes * TILES, LANES), scratch(2, planes * NG, LANES)
    terms = pl.pallas_call(
        kernel,
        out_shape=jax.ShapeDtypeStruct(flat.shape, jnp.float32),
        in_specs=[hbm] * 5,
        out_specs=vmem,
        scratch_shapes=[
            scratch(*flat.shape), *(scratch(*t.shape) for t in constants),
            *(pltpu.VMEM((2, *t.shape), jnp.bfloat16) for t in constants),
            as_it_lies, padded, as_it_lies, padded, padded,
            main, main, main, main, rest, rest,
            scratch(NG, 5 * LANES), as_it_lies, as_it_lies,
            pltpu.SemaphoreType.DMA((5,)),
            pltpu.SemaphoreType.DMA((4,)), pltpu.SemaphoreType.DMA((4,)),
            pltpu.SemaphoreType.DMA((5, SLABS)), pltpu.SemaphoreType.DMA((5, SLABS)),
            pltpu.SemaphoreType.DMA((5,)), pltpu.SemaphoreType.REGULAR,
        ],
        compiler_params=pltpu.CompilerParams(
            collective_id=0, has_side_effects=True, vmem_limit_bytes=32 * 1024 * 1024
        ),
    )(*(pltpu.with_memory_space_constraint(a, pltpu.HBM) for a in (flat, *map(jnp.asarray, constants))))
    terms = terms.reshape(planes, TILES, count, LANES).transpose(2, 0, 1, 3)
    return terms.reshape(count, planes, cells)


def solution(mesh):
    spec = P("blk", "grid", None)
    return jax.shard_map(on_device, mesh=mesh, in_specs=(spec,), out_specs=spec, check_vma=False)
```

```python
import math

import jax
import jax.numpy as jnp
import numpy as np
from jax import lax
from jax.experimental import pallas as pl
from jax.experimental.pallas import tpu as pltpu
from jax.sharding import PartitionSpec as P

NG = 96
LANES = 128
HALF = LANES // 2
BOX_LENGTH = 37.25
OMEGA = 0.11
SLABS = 32
PLANES = 3
TILES = NG * NG // LANES
TURN = 4
TURNS = NG // TURN
MAIN = 4 * PLANES
REST = PLANES
MAIN_PITCH = 16
REST_PITCH = 8
MESH = pl.DeviceIdType.MESH
FAR_FIRST = sorted(range(1, SLABS), key=lambda k: abs(k - SLABS // 2))


def tables():
    index = np.arange(NG)
    angle = 2.0 * np.pi / NG * ((index[:, None] * index[None, :]) % NG)
    hartley = np.cos(angle) + np.sin(angle)
    by_slab = (np.arange(PLANES)[:, None] + PLANES * np.arange(SLABS)[None, :]).reshape(-1)
    by_turn = (np.arange(TURN)[:, None] + TURN * np.arange(TURNS)[None, :]).reshape(-1)
    dealt = hartley[by_slab][:, by_turn]
    packed = np.zeros((2 * NG, 2 * LANES))
    for i in range(2):
        packed[i * NG : (i + 1) * NG, i * LANES : i * LANES + NG] = hartley
    to_spectrum = np.concatenate([packed.T, packed.T[:, LANES : 2 * NG]], axis=1)
    from_spectrum = np.concatenate([packed, np.zeros((2 * LANES - 2 * NG, 2 * LANES))], axis=0)
    return tuple(t.astype(np.float32) for t in (dealt, dealt.T, to_spectrum, from_spectrum))


def halves(value):
    high = value.astype(jnp.bfloat16)
    low = (value - high.astype(jnp.float32)).astype(jnp.bfloat16)
    return high, low


def dot(a, b):
    return jnp.dot(a, b, preferred_element_type=jnp.float32)


def times_table(value, table):
    high, low = halves(value)
    return dot(high, table[0]) + (dot(low, table[0]) + dot(high, table[1]))


def table_times(table, value):
    high, low = halves(value)
    return dot(table[0], high) + (dot(table[0], low) + dot(table[1], high))


def signed(index):
    return jnp.where(index < NG - NG // 2, index, index - NG).astype(jnp.float32) * jnp.float32(
        2.0 * math.pi / BOX_LENGTH
    )


def screen_tile(kx, ky, kz):
    squared = signed(kx) ** 2 + signed(ky) ** 2 + signed(kz) ** 2
    safe = jnp.where(squared > 0, squared, jnp.float32(1.0))
    value = 4.0 * math.pi / safe * (1.0 - jnp.exp(-safe / (4.0 * OMEGA * OMEGA)))
    value = jnp.where(squared > 0, value, jnp.float32(math.pi / (OMEGA * OMEGA)))
    return value * jnp.float32(1.0 / (NG * NG * NG))


def turned(value, by=HALF):
    return pltpu.roll(value, by, 1)


def unpacked(flat, x):
    a, b, c = (flat[pl.ds(x * TILES + k, TURNS, stride=3), :] for k in range(3))
    lane = lax.broadcasted_iota(jnp.int32, a.shape, 1)
    second = jnp.where(lane < 32, turned(a, 32), turned(b, 32))
    third = jnp.where(lane < HALF, turned(b), turned(c))
    return jnp.concatenate([a, second, third, turned(c, 96)], axis=0)


def packed_rows(plane):
    first, second, third, fourth = (plane[k * TURNS : (k + 1) * TURNS] for k in range(TURN))
    lane = lax.broadcasted_iota(jnp.int32, first.shape, 1)
    second, third = turned(second, 96), turned(third)
    return (
        jnp.where(lane < NG, first, second),
        jnp.where(lane < HALF, second, third),
        jnp.where(lane < 32, third, turned(fourth, 32)),
    )


def put(ref, row, value):
    pitch = ref.shape[1]
    ref.reshape(SLABS * pitch, LANES)[pl.ds(row, SLABS, stride=pitch), :] = value


def get(ref, row):
    pitch = ref.shape[1]
    return ref.reshape(SLABS * pitch, LANES)[pl.ds(row, SLABS, stride=pitch), :]


def kernel(
    orbitals, dealt_in, dealt_t_in, to_spectrum_in, from_spectrum_in, out,
    raw, dealt_raw, dealt_t_raw, to_spectrum_raw, from_spectrum_raw,
    dealt, dealt_t, to_spectrum, from_spectrum,
    own_flat, own, partner_flat, partner, to_own,
    sent, arrived, screened, returned, screened_rest, returned_rest,
    screen, terms, terms_in,
    load_sem, swap_send, swap_recv, send_sem, recv_sem, local_sem, turn_sem,
):
    me = lax.axis_index("grid")
    block = lax.axis_index("blk")
    blocks = lax.axis_size("blk")
    after = lax.rem(block + 1, blocks)
    before = lax.rem(block + blocks - 1, blocks)
    peers = {k: lax.rem(me + k, SLABS) for k in FAR_FIRST}

    barrier = pltpu.get_barrier_semaphore()
    for k in FAR_FIRST:
        pl.semaphore_signal(barrier, inc=1, device_id={"grid": peers[k]}, device_id_type=MESH)
    for neighbour in (before, after):
        pl.semaphore_signal(barrier, inc=1, device_id={"blk": neighbour}, device_id_type=MESH)

    loads = [
        pltpu.make_async_copy(source, target, load_sem.at[k])
        for k, (source, target) in enumerate(
            [
                (orbitals, raw),
                (to_spectrum_in, to_spectrum_raw),
                (dealt_in, dealt_raw),
                (dealt_t_in, dealt_t_raw),
                (from_spectrum_in, from_spectrum_raw),
            ]
        )
    ]
    for load in loads:
        load.start()

    shape = (NG, LANES)
    row = lax.broadcasted_iota(jnp.int32, shape, 0)
    turn = (row >= TURNS).astype(jnp.int32) + (row >= 2 * TURNS) + (row >= 3 * TURNS)
    kx = TURN * (row - TURNS * turn) + turn
    lane = lax.broadcasted_iota(jnp.int32, shape, 1)
    low_half = lane < HALF
    first = PLANES * me
    for r in range(PLANES):
        screen[:, r * LANES : (r + 1) * LANES] = screen_tile(
            kx, jnp.full(shape, first + r, jnp.int32), jnp.where(lane < NG, lane, lane - NG)
        )
    kz = jnp.where(low_half, lane, lane - HALF) + (LANES - NG)
    screen[:, 3 * LANES : 4 * LANES] = screen_tile(kx, jnp.where(low_half, first, first + 1), kz)
    screen[:, 4 * LANES : 5 * LANES] = screen_tile(kx, jnp.full(shape, first + 2, jnp.int32), kz)

    loads[0].wait()
    for i in range(2):
        own_flat[i] = raw[pl.ds(i, PLANES * TILES, stride=2), :]
        for x in range(PLANES):
            own[i, x * NG : (x + 1) * NG] = unpacked(own_flat.at[i], x)
    for load in loads[1:]:
        load.wait()
    for source, target in (
        (to_spectrum_raw, to_spectrum),
        (dealt_raw, dealt),
        (dealt_t_raw, dealt_t),
        (from_spectrum_raw, from_spectrum),
    ):
        target[0], target[1] = halves(source[...])

    pl.semaphore_wait(barrier, SLABS + 1)

    def swap(source, target, slot, whom):
        return pltpu.make_async_remote_copy(
            src_ref=source, dst_ref=target, send_sem=swap_send.at[slot], recv_sem=swap_recv.at[slot],
            device_id={"blk": whom}, device_id_type=MESH,
        )

    orbital_swaps = [swap(own_flat.at[j], partner_flat.at[j], j, after) for j in range(2)]
    for copy in orbital_swaps:
        copy.start()

    def message(source, target, rows, slot, k, origin, peer):
        return pltpu.make_async_remote_copy(
            src_ref=source.at[peer, pl.ds(0, rows)],
            dst_ref=target.at[origin, pl.ds(0, rows)],
            send_sem=send_sem.at[slot, k],
            recv_sem=recv_sem.at[slot, origin],
            device_id={"grid": peer},
            device_id_type=MESH,
        )

    def stay(source, target, rows, slot):
        return pltpu.make_async_copy(source.at[me], target.at[me], local_sem.at[slot])

    def scatter(*job):
        source, target, rows, slot = job
        for k in FAR_FIRST:
            message(*job, k, me, peers[k]).start()
        stay(*job).start()

    def gather(*job):
        for k in FAR_FIRST:
            message(*job, k, peers[k], peers[k]).wait_recv()
        stay(*job).wait()

    def drain(*job):
        for k in FAR_FIRST:
            message(*job, k, me, peers[k]).wait_send()

    out_jobs = [(sent.at[j], arrived.at[j], MAIN + REST * j, j) for j in range(2)]
    back_jobs = [(screened.at[j], returned.at[j], MAIN, 2 + j) for j in range(2)]
    back_rest = (screened_rest, returned_rest, REST, 4)

    in_low = lax.broadcasted_iota(jnp.int32, (SLABS, LANES), 1) < HALF

    thirds = []
    for j in range(2):
        orbital_swaps[j].wait_recv()
        for x in range(PLANES):
            plane = pl.ds(x * NG, NG)
            other = unpacked(partner_flat.at[j], x)
            partner[j, plane] = other
            density = jnp.concatenate([own[0, plane] * other, own[1, plane] * other], axis=1)
            spectrum = table_times(dealt, times_table(density, to_spectrum))
            rest = []
            for r in range(PLANES):
                rows = spectrum[r * SLABS : (r + 1) * SLABS]
                put(sent.at[j], x * 4 + r, rows[:, :LANES])
                rest.append(rows[:, LANES:])
            put(sent.at[j], x * 4 + 3, jnp.where(in_low, rest[0], rest[1]))
            if j == 0:
                thirds.append(rest[2])
            else:
                put(sent.at[j], MAIN + x, jnp.where(in_low, thirds[x], rest[2]))
        scatter(*out_jobs[j])

    def along_x(source, start, width, tile):
        columns = []
        for c in range(width):
            rows = [get(source, start + x * width + c) for x in range(PLANES)]
            columns.append(jnp.concatenate(rows, axis=0))
        spectrum = table_times(dealt_t, jnp.concatenate(columns, axis=1))
        return table_times(dealt, spectrum * screen[:, tile * LANES : (tile + width) * LANES])

    def deal(target, back, width):
        for x in range(PLANES):
            rows = back[x * SLABS : (x + 1) * SLABS]
            for c in range(width):
                put(target, x * width + c, rows[:, c * LANES : (c + 1) * LANES])

    gather(*out_jobs[0])
    deal(screened.at[0], along_x(arrived.at[0], 0, 4, 0), 4)
    scatter(*back_jobs[0])
    gather(*out_jobs[1])
    deal(screened_rest, along_x(arrived.at[1], MAIN, 1, 4), 1)
    scatter(*back_rest)
    deal(screened.at[1], along_x(arrived.at[1], 0, 4, 0), 4)
    odd = lax.rem(block, 2) == 1

    @pl.when(odd)
    def _():
        pl.semaphore_wait(turn_sem, 1)

    scatter(*back_jobs[1])

    @pl.when(jnp.logical_not(odd))
    def _():
        for k in FAR_FIRST[:24]:
            message(*back_jobs[1], k, me, peers[k]).wait_send()
        pl.semaphore_signal(turn_sem, inc=1, device_id={"blk": after}, device_id_type=MESH)

    for copy in orbital_swaps:
        copy.wait_send()
    for job in out_jobs:
        drain(*job)

    term_swaps = [swap(terms.at[j], terms_in.at[j], 2 + j, before) for j in range(2)]
    gather(*back_rest)
    for j in range(2):
        gather(*back_jobs[j])
        columns = []
        for x in range(PLANES):
            main = [get(returned.at[j], x * 4 + r) for r in range(PLANES)]
            columns.append(jnp.concatenate(main, axis=0))
            both = get(returned.at[j], x * 4 + 3)
            last = get(returned_rest, x)
            if j == 1:
                last = turned(last)
            columns.append(jnp.concatenate([both, turned(both), last], axis=0))
        side_by_side = table_times(dealt_t, jnp.concatenate(columns, axis=1))
        spectra = [side_by_side[:, 2 * x * LANES : 2 * (x + 1) * LANES] for x in range(PLANES)]
        potentials = times_table(jnp.concatenate(spectra, axis=0), from_spectrum)
        planes = []
        for x in range(PLANES):
            plane = pl.ds(x * NG, NG)
            potential = potentials[x * NG : (x + 1) * NG]
            parts = [potential[:, :LANES], potential[:, LANES:]]
            planes.append(parts)
            term = -(parts[0] * own[0, plane] + parts[1] * own[1, plane])
            for k, value in enumerate(packed_rows(term)):
                terms[j, pl.ds(x * TILES + k, TURNS, stride=3), :] = value
        term_swaps[j].start()
        for x in range(PLANES):
            plane = pl.ds(x * NG, NG)
            for i in range(2):
                mine = planes[x][i] * partner[j, plane]
                if j == 0:
                    to_own[i, plane] = -mine
                else:
                    to_own[i, plane] = to_own[i, plane] - mine
        if j == 0:
            drain(*back_jobs[0])
            drain(*back_rest)
    for k in FAR_FIRST[24:]:
        message(*back_jobs[1], k, me, peers[k]).wait_send()

    @pl.when(odd)
    def _():
        for k in FAR_FIRST[:24]:
            message(*back_jobs[1], k, me, peers[k]).wait_send()

    for i in range(2):
        term_swaps[i].wait_recv()
        for x in range(PLANES):
            for k, value in enumerate(packed_rows(to_own[i, pl.ds(x * NG, NG)])):
                theirs = terms_in[i, pl.ds(x * TILES + k, TURNS, stride=3), :]
                out[pl.ds((x * TILES + k) * 2 + i, TURNS, stride=6), :] = value + theirs

    for copy in term_swaps:
        copy.wait_send()


def on_device(orbitals):
    count, planes, cells = orbitals.shape
    flat = orbitals.reshape(count, planes, TILES, LANES).transpose(1, 2, 0, 3)
    flat = flat.reshape(planes * TILES * count, LANES)
    vmem = pl.BlockSpec(memory_space=pltpu.VMEM)
    hbm = pl.BlockSpec(memory_space=pltpu.HBM)
    constants = tables()

    def scratch(*shape):
        return pltpu.VMEM(shape, jnp.float32)

    main, rest = scratch(2, SLABS, MAIN_PITCH, LANES), scratch(SLABS, REST_PITCH, LANES)
    as_it_lies, padded = scratch(2, planes * TILES, LANES), scratch(2, planes * NG, LANES)
    terms = pl.pallas_call(
        kernel,
        out_shape=jax.ShapeDtypeStruct(flat.shape, jnp.float32),
        in_specs=[hbm] * 5,
        out_specs=vmem,
        scratch_shapes=[
            scratch(*flat.shape), *(scratch(*t.shape) for t in constants),
            *(pltpu.VMEM((2, *t.shape), jnp.bfloat16) for t in constants),
            as_it_lies, padded, as_it_lies, padded, padded,
            main, main, main, main, rest, rest,
            scratch(NG, 5 * LANES), as_it_lies, as_it_lies,
            pltpu.SemaphoreType.DMA((5,)),
            pltpu.SemaphoreType.DMA((4,)), pltpu.SemaphoreType.DMA((4,)),
            pltpu.SemaphoreType.DMA((5, SLABS)), pltpu.SemaphoreType.DMA((5, SLABS)),
            pltpu.SemaphoreType.DMA((5,)), pltpu.SemaphoreType.REGULAR,
        ],
        compiler_params=pltpu.CompilerParams(
            collective_id=0, has_side_effects=True, vmem_limit_bytes=32 * 1024 * 1024
        ),
    )(*(pltpu.with_memory_space_constraint(a, pltpu.HBM) for a in (flat, *map(jnp.asarray, constants))))
    terms = terms.reshape(planes, TILES, count, LANES).transpose(2, 0, 1, 3)
    return terms.reshape(count, planes, cells)


def solution(mesh):
    spec = P("blk", "grid", None)
    return jax.shard_map(on_device, mesh=mesh, in_specs=(spec,), out_specs=spec, check_vma=False)
```
